32 devices in a mesh: dp: 8 (over z, y), expert: 4 (over x, core).
Axes of the slice: x: 2, y: 2, z: 4, core: 2. Of those that a mesh axis runs over, the one named last changes fastest.
Arguments:
- local_grads: bfloat16 [4, 8, 1024, 3584], P('expert', 'dp')
- momentum: float32 [4, 1024, 3584], P('expert', None, 'dp'), may hold values from -6 to 6
Outputs:
- new_momentum: float32 [4, 1024, 3584], P('expert', None, 'dp')
- update: float32 [4, 1024, 3584], P('expert', None, 'dp')
The draws below stay inside these ranges and needn't reach their ends.
All inputs are finite; a program needn't handle non-finite values.
Results may differ from the reference program's by a relative error of at most 0.0003.
Values sent between devices are 32-bit elements; how exact they have to be, the bound alone decides.
No kernel may reach another device: no remote copies, remote signals or barrier semaphores. Data moves between devices by JAX's collectives and lax.ppermute only.
A program may use at most 128 MiB of HBM per device.

```python
import math
import jax
import jax.numpy as jnp
from jax import lax

HID = 1024
WID = 3584
ITERS = 3
GROUPS = 4
REPLICAS = 8


def draw_local_grads(key, part):
    keys = jax.random.split(jax.random.fold_in(key, 17), 3)
    top_row = 10.0
    row_scale = jnp.exp(jax.random.uniform(keys[0], (GROUPS, 1, HID, 1), jnp.float32) * math.log(top_row))
    col_scale = jnp.exp(jax.random.uniform(keys[1], (GROUPS, 1, 1, WID), jnp.float32) * math.log(10.0))
    col_ramp = jnp.exp(jnp.arange(WID, dtype=jnp.float32) / max(WID - 1, 1) * math.log(3.0))
    group_ramp = jnp.exp(jnp.arange(GROUPS, dtype=jnp.float32) / max(GROUPS - 1, 1) * math.log(3.0))
    shaped = row_scale * col_scale * col_ramp[None, None, None, :] * group_ramp[:, None, None, None] * 0.05
    values = jax.random.normal(keys[2], (GROUPS, REPLICAS, HID, WID), jnp.float32)
    return (values * shaped).astype(jnp.bfloat16)


def block_scale(own_key, shape, cuts, low, high):
    level = 1.0
    for dim, blocks in cuts:
        steps = jax.random.uniform(jax.random.fold_in(jax.random.fold_in(own_key, 6), dim), (blocks,), jnp.float32, low / len(cuts), high / len(cuts))
        level = level * jnp.repeat(jnp.exp(steps), shape[dim] // blocks).reshape((-1,) + (1,) * (len(shape) - 1 - dim))
    return level


def gaussian(key, shape, spread, limit, shards=(), held_as=jnp.bfloat16):
    array = jax.random.normal(key, shape, jnp.float32) * spread
    if len(shards) > 0:
        array = block_scale(key, shape, shards, -0.22, 0.18) * array
    return jnp.clip(array, min=-limit, max=limit).astype(held_as)


def setup_inputs(seed: int = 0) -> dict:
    splits = jax.random.split(jax.random.key(seed), 3)
    return {
        "local_grads": draw_local_grads(jax.random.fold_in(splits[2], 71), 0),
        "momentum": gaussian(splits[1], (GROUPS, HID, WID), 1.0, 6.0, ((0, 4), (2, 8)), jnp.float32),
    }


first_coef = 3.4445
second_coef = -4.775
third_coef = 2.0315
momentum_decay = 0.95

def precise(left, right):
    return jnp.dot(left, right, precision=lax.Precision.HIGHEST, preferred_element_type=jnp.float32)

def orthogonal(blend):
    iterate = blend / (jnp.sqrt(jnp.sum(blend * blend)) + 1e-07)
    for number in range(ITERS):
        gram = precise(iterate, iterate.T)
        poly = second_coef * gram + third_coef * precise(gram, gram)
        iterate = first_coef * iterate + precise(poly, iterate)
    return iterate * (0.2 * math.sqrt(max(HID, WID)))

def reference(local_grads, momentum):
    grads = lax.optimization_barrier(jnp.sum(local_grads, axis=1, dtype=jnp.float32))
    root_mean = jnp.sqrt(jnp.mean(grads * grads) + 1e-06)
    factor = jnp.minimum(1.0, 1.0 / root_mean)
    clipped = factor * grads
    new_momentum = momentum_decay * momentum + clipped
    blend = clipped + momentum_decay * new_momentum
    update = lax.map(orthogonal, blend)
    return (new_momentum, update)
```

```python
import math

import jax
import jax.numpy as jnp
from jax import lax
from jax.sharding import PartitionSpec as P

ITERS = 3

first_coef = 3.4445
second_coef = -4.775
third_coef = 2.0315
momentum_decay = 0.95


def product(left, right):
    return jnp.dot(left, right, precision=lax.Precision.HIGH, preferred_element_type=jnp.float32)


def body(local_grads, momentum):
    hid, wid = local_grads.shape[2:]
    grads = lax.psum_scatter(
        local_grads[0, 0].astype(jnp.float32), "dp", scatter_dimension=1, tiled=True
    )
    count = hid * wid * lax.axis_size("expert")
    total_sq = lax.psum(jnp.sum(grads * grads), ("dp", "expert"))
    root_mean = jnp.sqrt(total_sq / count + 1e-06)
    factor = jnp.minimum(1.0, 1.0 / root_mean)
    clipped = factor * grads
    new_momentum = momentum_decay * momentum[0] + clipped
    blend = clipped + momentum_decay * new_momentum
    gram = lax.psum(product(blend, blend.T), "dp")
    norm = jnp.sqrt(jnp.trace(gram)) + 1e-07
    iterate = blend / norm
    gram = gram / (norm * norm)
    eye = jnp.eye(hid, dtype=jnp.float32)
    for number in range(ITERS):
        poly = first_coef * eye + second_coef * gram + third_coef * product(gram, gram)
        iterate = product(poly, iterate)
        if number < ITERS - 1:
            gram = product(product(gram, poly), poly)
    update = iterate * (0.2 * math.sqrt(max(hid, wid)))
    return (new_momentum[None], update[None])


def solution(mesh):
    return jax.shard_map(
        body,
        mesh=mesh,
        in_specs=(P("expert", "dp", None, None), P("expert", None, "dp")),
        out_specs=(P("expert", None, "dp"), P("expert", None, "dp")),
        check_vma=False,
    )
```

```python
import math

import jax
import jax.numpy as jnp
from jax import lax
from jax.sharding import PartitionSpec as P

ITERS = 3
STREAMS = 4
FOLD = 128

first_coef = 3.4445
second_coef = -4.775
third_coef = 2.0315
momentum_decay = 0.95


def product(left, right):
    return jnp.dot(left, right, precision=lax.Precision.HIGH, preferred_element_type=jnp.float32)


def ring_order(size):
    return list(range(0, size, 2)) + list(range(1, size, 2))[::-1]


class Ring:
    def __init__(self, axis):
        self.axis = axis
        self.size = lax.axis_size(axis)
        self.order = ring_order(self.size)
        cycle = self.order + self.order
        table = [cycle[cycle.index(index):][:self.size] for index in range(self.size)]
        self.owners = jnp.array(table, jnp.int32)[lax.axis_index(axis)]

    def owner(self, offset):
        return self.owners[offset % self.size]

    def send(self, value, way):
        pairs = [(self.order[p], self.order[(p + way) % self.size]) for p in range(self.size)]
        return lax.ppermute(value, self.axis, pairs)


def ring_sum_scatter(ring, terms):
    ways = [1 if k % 2 == 0 else -1 for k in range(len(terms))]

    def local(k, offset):
        return lax.dynamic_index_in_dim(terms[k], ring.owner(offset), 0, keepdims=False).astype(jnp.float32)

    held = [local(k, -way) for k, way in enumerate(ways)]
    for step in range(ring.size - 1):
        for k, way in enumerate(ways):
            held[k] = ring.send(held[k], way) + local(k, -way * (step + 2))
    return held


def direct_sum(value, axis):
    size = lax.axis_size(axis)
    total = value
    for shift in range(1, size):
        total = total + lax.ppermute(value, axis, [(p, (p + shift) % size) for p in range(size)])
    return total


def fold(gram):
    size = gram.shape[0]
    parts = size // FOLD
    rows = []
    for p in range(parts // 2):
        q = parts - 1 - p
        rows.append(jnp.concatenate(
            [gram[p * FOLD:(p + 1) * FOLD, p * FOLD:], gram[q * FOLD:(q + 1) * FOLD, q * FOLD:]], axis=1
        ))
    return jnp.concatenate(rows, axis=0)


def unfold(packed, size):
    parts = size // FOLD
    blocks = {}
    for p in range(parts // 2):
        q = parts - 1 - p
        row = packed[p * FOLD:(p + 1) * FOLD]
        for c in range(p, parts):
            blocks[p, c] = row[:, (c - p) * FOLD:(c - p + 1) * FOLD]
        for c in range(q, parts):
            at = parts - p + c - q
            blocks[q, c] = row[:, at * FOLD:(at + 1) * FOLD]
    return jnp.concatenate([
        jnp.concatenate([blocks[r, c] if c >= r else blocks[c, r].T for c in range(parts)], axis=1)
        for r in range(parts)
    ], axis=0)


def body(local_grads, momentum):
    hid, wid = local_grads.shape[2:]
    ring = Ring("dp")
    rows = hid // STREAMS
    terms = [
        local_grads[0, 0, k * rows:(k + 1) * rows].reshape(rows, ring.size, wid // ring.size).transpose(1, 0, 2)
        for k in range(STREAMS)
    ]
    grads = jnp.concatenate(ring_sum_scatter(ring, terms), axis=0)
    count = hid * wid * lax.axis_size("expert")
    total_sq = direct_sum(direct_sum(jnp.sum(grads * grads).reshape(1), "dp"), "expert")[0]
    root_mean = jnp.sqrt(total_sq / count + 1e-06)
    factor = jnp.minimum(1.0, 1.0 / root_mean)
    clipped = factor * grads
    new_momentum = momentum_decay * momentum[0] + clipped
    blend = clipped + momentum_decay * new_momentum
    gram = unfold(lax.psum(fold(product(blend, blend.T)), "dp"), hid)
    norm = jnp.sqrt(jnp.trace(gram)) + 1e-07
    iterate = blend / norm
    gram = gram / (norm * norm)
    eye = jnp.eye(hid, dtype=jnp.float32)
    for number in range(ITERS):
        poly = first_coef * eye + second_coef * gram + third_coef * product(gram, gram)
        iterate = product(poly, iterate)
        if number < ITERS - 1:
            gram = product(product(gram, poly), poly)
    update = iterate * (0.2 * math.sqrt(max(hid, wid)))
    return (new_momentum[None], update[None])


def solution(mesh):
    return jax.shard_map(
        body,
        mesh=mesh,
        in_specs=(P("expert", "dp", None, None), P("expert", None, "dp")),
        out_specs=(P("expert", None, "dp"), P("expert", None, "dp")),
        check_vma=False,
    )
```

```python
import functools
import math

import jax
import jax.numpy as jnp
from jax import lax
from jax.experimental import pallas as pl
from jax.experimental.pallas import tpu as pltpu
from jax.sharding import PartitionSpec as P

ITERS = 3
STREAMS = 4
FOLD = 128
BLOCK = 256
LANES = 128
VMEM_BYTES = 56 * 2**20

first_coef = 3.4445
second_coef = -4.775
third_coef = 2.0315
momentum_decay = 0.95
f32 = jnp.float32
bf16 = jnp.bfloat16


def ring_order(size):
    return list(range(0, size, 2)) + list(range(1, size, 2))[::-1]


class Ring:
    def __init__(self, axis):
        self.axis = axis
        self.size = lax.axis_size(axis)
        self.order = ring_order(self.size)
        cycle = self.order + self.order
        table = [cycle[cycle.index(index):][:self.size] for index in range(self.size)]
        self.owners = jnp.array(table, jnp.int32)[lax.axis_index(axis)]

    def owner(self, offset):
        return self.owners[offset % self.size]

    def send(self, value, way):
        pairs = [(self.order[p], self.order[(p + way) % self.size]) for p in range(self.size)]
        return lax.ppermute(value, self.axis, pairs)


def ring_sum_scatter(ring, terms):
    ways = [1 if k % 2 == 0 else -1 for k in range(len(terms))]

    def local(k, offset):
        return lax.dynamic_index_in_dim(terms[k], ring.owner(offset), 0, keepdims=False).astype(jnp.float32)

    held = [local(k, -way) for k, way in enumerate(ways)]
    for step in range(ring.size - 1):
        for k, way in enumerate(ways):
            held[k] = ring.send(held[k], way) + local(k, -way * (step + 2))
    return held


def direct_sum(value, axis):
    size = lax.axis_size(axis)
    return sum(
        (lax.ppermute(value, axis, [(p, (p + shift) % size) for p in range(size)]) for shift in range(1, size)),
        value,
    )


def relayout_kernel(source, target):
    owners, _, columns = target.shape
    for j in range(owners):
        target[j] = source[0, 0, :, j * columns:(j + 1) * columns]


def relayout(local_grads, owners, stream, rows):
    wid = local_grads.shape[3]
    step = min(64, rows)
    return pl.pallas_call(
        relayout_kernel,
        grid=(rows // step,),
        in_specs=[pl.BlockSpec((1, 1, step, wid), lambda i: (0, 0, stream * (rows // step) + i, 0))],
        out_specs=pl.BlockSpec((owners, step, wid // owners), lambda i: (0, i, 0)),
        out_shape=jax.ShapeDtypeStruct((owners, rows, wid // owners), local_grads.dtype),
        compiler_params=pltpu.CompilerParams(vmem_limit_bytes=VMEM_BYTES),
        cost_estimate=pl.CostEstimate(flops=0, bytes_accessed=4 * rows * wid, transcendentals=0),
    )(local_grads)


def split(value):
    high = value.astype(bf16)
    return high, (value - high.astype(f32)).astype(bf16)


def dot(left, right, contract):
    return lax.dot_general(left, right, ((contract[:1], contract[1:]), ((), ())), preferred_element_type=f32)


def dot3(left, right, contract=(1, 0)):
    (lh, ll), (rh, rl) = left, right
    return dot(lh, rh, contract) + (dot(lh, rl, contract) + dot(ll, rh, contract))


def folded(parts):
    for r in range(parts):
        for c in range(r, parts):
            if r < parts // 2:
                yield r, c, r, c - r
            else:
                yield r, c, parts - 1 - r, parts + 1 - (parts - c)


def at(block, size):
    return slice(block * size, (block + 1) * size)


def blend_gram_kernel(factor, momentum, *refs):
    grads = refs[:STREAMS]
    new_momentum, blend, packed, high, low = refs[STREAMS:]
    hid, columns = blend.shape
    scale = factor[0:1, 0:1]
    rows = hid // STREAMS
    if high.shape[1] > columns:
        high[:, columns:] = jnp.zeros((hid, high.shape[1] - columns), bf16)
        low[:, columns:] = jnp.zeros((hid, high.shape[1] - columns), bf16)
    for k in range(STREAMS):
        where = at(k, rows)
        clipped = scale * grads[k][...]
        moved = momentum_decay * momentum[0, where, :] + clipped
        mixed = clipped + momentum_decay * moved
        new_momentum[0, where, :] = moved
        blend[where, :] = mixed
        high[where, :columns], low[where, :columns] = split(mixed)
    place = {(r, c): (u, v) for r, c, u, v in folded(hid // FOLD)}
    per = BLOCK // FOLD
    for r in range(hid // BLOCK):
        for c in range(r, hid // BLOCK):
            value = dot3((high[at(r, BLOCK), :], low[at(r, BLOCK), :]),
                         (high[at(c, BLOCK), :], low[at(c, BLOCK), :]), (1, 1))
            for i in range(per):
                for j in range(per):
                    if (r * per + i, c * per + j) in place:
                        u, v = place[r * per + i, c * per + j]
                        packed[at(u, FOLD), at(v, FOLD)] = value[at(i, FOLD), at(j, FOLD)]


def blend_gram(factor, momentum, grads):
    _, hid, columns = momentum.shape
    padded = -(-columns // LANES) * LANES
    shapes = [
        jax.ShapeDtypeStruct(momentum.shape, f32),
        jax.ShapeDtypeStruct((hid, columns), f32),
        jax.ShapeDtypeStruct((hid // 2, hid + FOLD), f32),
    ]
    vmem = pl.BlockSpec(memory_space=pltpu.VMEM)
    return pl.pallas_call(
        blend_gram_kernel,
        in_specs=[vmem] * (2 + STREAMS),
        out_specs=[vmem] * 3,
        out_shape=shapes,
        scratch_shapes=[pltpu.VMEM((hid, padded), bf16)] * 2,
        compiler_params=pltpu.CompilerParams(vmem_limit_bytes=VMEM_BYTES),
    )(factor, momentum, *grads)


def chain_kernel(scale, packed, blend, update, gram, ah, al, ph, pll, th, tl, xh, xl, yh, yl, x32, y32):
    hid, columns = blend.shape
    parts = hid // FOLD
    blocks = hid // BLOCK
    pairs = [(r, c) for c in range(blocks) for r in range(c + 1)]
    per = BLOCK // FOLD
    place = {(r, c): (u, v) for r, c, u, v in folded(parts)}
    row = lax.broadcasted_iota(jnp.int32, (BLOCK, BLOCK), 0)
    eye = (row == lax.broadcasted_iota(jnp.int32, (BLOCK, BLOCK), 1)).astype(f32)

    def piece(r, c):
        u, v = place[r, c]
        return packed[at(u, FOLD), at(v, FOLD)]

    small = eye[:FOLD, :FOLD]
    diagonal = sum(piece(r, r) * small for r in range(parts))
    trace = jnp.sum(jnp.sum(diagonal, axis=1, keepdims=True), axis=0, keepdims=True)
    inverse = 1.0 / (jnp.sqrt(trace) + 1e-07)
    inverse_sq = inverse * inverse

    def store(pair, r, c, value):
        for target, part in zip(pair, split(value)):
            target[at(r, BLOCK), at(c, BLOCK)] = part
            if r != c:
                target[at(c, BLOCK), at(r, BLOCK)] = part.T

    def symmetric(left, right, r, c):
        return dot3(tuple(m[at(r, BLOCK), :] for m in left), tuple(m[:, at(c, BLOCK)] for m in right))

    def apply(left, right, r):
        return dot3(tuple(m[at(r, BLOCK), :] for m in left), tuple(m[...] for m in right))

    a, p, t = (ah, al), (ph, pll), (th, tl)
    x, y = (xh, xl), (yh, yl)

    for r, c in pairs:
        rows = []
        for i in range(per):
            line = []
            for j in range(per):
                u, v = r * per + i, c * per + j
                line.append(piece(u, v) if u <= v else piece(v, u).T)
            rows.append(jnp.concatenate(line, axis=1))
        value = jnp.concatenate(rows, axis=0) * inverse_sq
        gram[at(r, BLOCK), at(c, BLOCK)] = value
        store(a, r, c, value)
    for r in range(blocks):
        for target, part in zip(x, split(blend[at(r, BLOCK), :] * inverse)):
            target[at(r, BLOCK), :] = part

    for number in range(ITERS - 1):
        for r, c in pairs:
            value = third_coef * symmetric(a, a, r, c) + second_coef * gram[at(r, BLOCK), at(c, BLOCK)]
            store(p, r, c, value + first_coef * eye if r == c else value)
        for r in range(blocks):
            value = apply(p, x, r)
            if number == ITERS - 2:
                x32[at(r, BLOCK), :] = value
            for target, part in zip(y, split(value)):
                target[at(r, BLOCK), :] = part
        x, y = y, x
        for r, c in pairs:
            store(t, r, c, symmetric(a, p, r, c))
        for r, c in pairs:
            value = symmetric(t, p, r, c)
            store(a, r, c, value)
            if number < ITERS - 2:
                gram[at(r, BLOCK), at(c, BLOCK)] = value
    for r in range(blocks):
        value = apply(a, x, r)
        y32[at(r, BLOCK), :] = value
        for target, part in zip(y, split(value)):
            target[at(r, BLOCK), :] = part
    for r in range(blocks):
        where = at(r, BLOCK)
        value = first_coef * x32[where, :] + second_coef * y32[where, :] + third_coef * apply(a, y, r)
        update[0, where, :] = value * scale


def chain(packed, blend, scale):
    hid, columns = blend.shape
    vmem = pl.BlockSpec(memory_space=pltpu.VMEM)
    square, slab = pltpu.VMEM((hid, hid), bf16), pltpu.VMEM((hid, columns), bf16)
    return pl.pallas_call(
        functools.partial(chain_kernel, scale),
        in_specs=[vmem] * 2,
        out_specs=vmem,
        out_shape=jax.ShapeDtypeStruct((1, hid, columns), f32),
        scratch_shapes=[pltpu.VMEM((hid, hid), f32)] + [square] * 6 + [slab] * 4
        + [pltpu.VMEM((hid, columns), f32)] * 2,
        compiler_params=pltpu.CompilerParams(vmem_limit_bytes=VMEM_BYTES),
    )(packed, blend)


def body(local_grads, momentum):
    hid, wid = local_grads.shape[2:]
    ring = Ring("dp")
    rows = hid // STREAMS
    terms = [relayout(local_grads, ring.size, k, rows) for k in range(STREAMS)]
    grads = ring_sum_scatter(ring, terms)
    squares = sum(jnp.sum(part * part) for part in grads)
    total_sq = direct_sum(direct_sum(jnp.full((8, LANES), squares), "dp"), "expert")
    count = hid * wid * lax.axis_size("expert")
    factor = jnp.minimum(1.0, 1.0 / jnp.sqrt(total_sq / count + 1e-06))
    new_momentum, blend, packed = blend_gram(factor, momentum, grads)
    packed = lax.psum(packed, "dp")
    update = chain(packed, blend, 0.2 * math.sqrt(max(hid, wid)))
    return (new_momentum, update)


def solution(mesh):
    return jax.shard_map(
        body,
        mesh=mesh,
        in_specs=(P("expert", "dp", None, None), P("expert", None, "dp")),
        out_specs=(P("expert", None, "dp"), P("expert", None, "dp")),
        check_vma=False,
    )
```

```python
import functools
import math

import jax
import jax.numpy as jnp
from jax import lax
from jax.experimental import pallas as pl
from jax.experimental.pallas import tpu as pltpu
from jax.sharding import PartitionSpec as P

ITERS = 3
STREAMS = 4
FOLD = 128
BLOCK = 256
LANES = 128
MIB = 2**20

first_coef = 3.4445
second_coef = -4.775
third_coef = 2.0315
momentum_decay = 0.95
f32 = jnp.float32
bf16 = jnp.bfloat16


def ring_order(size):
    return list(range(0, size, 2)) + list(range(1, size, 2))[::-1]


class Ring:
    def __init__(self, axis):
        self.axis = axis
        self.size = lax.axis_size(axis)
        self.order = ring_order(self.size)
        cycle = self.order + self.order
        table = [cycle[cycle.index(index):][:self.size] for index in range(self.size)]
        self.owners = jnp.array(table, jnp.int32)[lax.axis_index(axis)]

    def owner(self, offset):
        return self.owners[offset % self.size]

    def send(self, value, way):
        pairs = [(self.order[p], self.order[(p + way) % self.size]) for p in range(self.size)]
        return lax.ppermute(value, self.axis, pairs)


def ring_sum_scatter(ring, ways, firsts, terms):
    held = list(firsts)
    for step in range(ring.size - 1):
        for k, way in enumerate(ways):
            term = lax.dynamic_index_in_dim(terms[k], ring.owner(-way * (step + 2)), 0, keepdims=False)
            held[k] = ring.send(held[k], way) + term.astype(f32)
    return held


class Line:
    def __init__(self, axis, size, stride):
        self.axis, self.size, self.stride = axis, size, stride
        self.digit = lax.rem(lax.div(lax.axis_index(axis), stride), size)

    def index(self, shift):
        return lax.rem(self.digit + shift + self.size, self.size)

    def send(self, value, shift):
        pairs = []
        for p in range(lax.axis_size(self.axis)):
            digit = p // self.stride % self.size
            pairs.append((p, p + ((digit + shift) % self.size - digit) * self.stride))
        return lax.ppermute(value, self.axis, pairs)

    def everyone(self, value):
        return [value] + [self.send(value, shift) for shift in range(1, self.size)]

    def sum(self, value):
        return sum(self.everyone(value)[1:], value)

    def sum_scatter(self, value):
        part = lambda shift: lax.dynamic_index_in_dim(value, self.index(shift), 0, keepdims=False)
        return sum([self.send(part(shift), shift) for shift in range(1, self.size)], part(0))

    def gather(self, value):
        result = jnp.zeros((self.size,) + value.shape, value.dtype)
        for shift, part in enumerate(self.everyone(value)):
            result = lax.dynamic_update_index_in_dim(result, part, self.index(-shift), 0)
        return result


def two_lines(axis):
    size = lax.axis_size(axis)
    inner = 2 if size % 2 == 0 else 1
    return Line(axis, size // inner, inner), Line(axis, inner, 1)


def all_sum(packed, axis):
    rows, width = packed.shape
    outer, inner = two_lines(axis)
    unit = rows // (outer.size * inner.size)
    small = max(1, 3 * unit // 8 // 4 * 4)
    large = unit - small
    cut = large * outer.size * inner.size
    one = inner.sum_scatter(packed[:cut].reshape(inner.size, outer.size * large, width))
    two = outer.sum_scatter(packed[cut:].reshape(outer.size, inner.size * small, width))
    one = outer.sum_scatter(one.reshape(outer.size, large, width))
    two = inner.sum_scatter(two.reshape(inner.size, small, width))
    one = outer.gather(one).reshape(outer.size * large, width)
    two = inner.gather(two).reshape(inner.size * small, width)
    pieces = inner.everyone(one) + outer.everyone(two)
    starts = [inner.index(-s) * one.shape[0] for s in range(inner.size)]
    starts += [cut + outer.index(-s) * two.shape[0] for s in range(outer.size)]
    return pieces, jnp.stack(starts).astype(jnp.int32)


def transpose_kernel(owner, source, target, first):
    wid = source.shape[3]
    columns = first.shape[0]
    step = 512
    for c in range(0, wid, step):
        width = min(step, wid - c)
        target[c:c + width, :] = source[0, 0, :, c:c + width].T
    first[...] = target[pl.ds(pl.multiple_of(owner[0] * columns, 16), columns), :].astype(f32)


def transposed(local_grads, owner, owners, stream, rows):
    wid = local_grads.shape[3]
    vmem = pl.BlockSpec(memory_space=pltpu.VMEM)
    target, first = pl.pallas_call(
        transpose_kernel,
        grid=(1,),
        in_specs=[
            pl.BlockSpec(memory_space=pltpu.SMEM),
            pl.BlockSpec((1, 1, rows, wid), lambda i: (0, 0, stream, 0)),
        ],
        out_specs=[vmem, vmem],
        out_shape=[
            jax.ShapeDtypeStruct((wid, rows), local_grads.dtype),
            jax.ShapeDtypeStruct((wid // owners, rows), f32),
        ],
        compiler_params=pltpu.CompilerParams(vmem_limit_bytes=14 * MIB),
        cost_estimate=pl.CostEstimate(flops=0, bytes_accessed=4 * rows * wid, transcendentals=0),
    )(owner.reshape(1), local_grads)
    return target.reshape(owners, wid // owners, rows), first


def split(value):
    high = value.astype(bf16)
    return high, (value - high.astype(f32)).astype(bf16)


def dot(left, right, contract):
    return lax.dot_general(left, right, ((contract[:1], contract[1:]), ((), ())), preferred_element_type=f32)


def dot3(left, right, contract=(1, 0)):
    (lh, ll), (rh, rl) = left, right
    return dot(lh, rh, contract) + (dot(lh, rl, contract) + dot(ll, rh, contract))


def folded(parts):
    for r in range(parts):
        for c in range(r, parts):
            if r < parts // 2:
                yield r, c, r, c - r
            else:
                yield r, c, parts - 1 - r, parts + 1 - (parts - c)


def at(block, size):
    return slice(block * size, (block + 1) * size)


def blend_gram_kernel(factor, momentum, *refs):
    grads = refs[:STREAMS]
    new_momentum, blend, packed, high, low, high_t, low_t = refs[STREAMS:]
    columns, hid = blend.shape
    scale = factor[0:1, 0:1]
    rows = hid // STREAMS
    if high.shape[0] > columns:
        for target in (high, low):
            target[columns:, :] = jnp.zeros((high.shape[0] - columns, hid), bf16)
        for target in (high_t, low_t):
            target[:, columns:] = jnp.zeros((hid, high.shape[0] - columns), bf16)
    for k in range(STREAMS):
        where = at(k, rows)
        clipped = scale * grads[k][...]
        moved = momentum_decay * momentum[:, where] + clipped
        mixed = clipped + momentum_decay * moved
        new_momentum[:, where] = moved
        blend[:, where] = mixed
        for target, turned, part in zip((high, low), (high_t, low_t), split(mixed)):
            target[:columns, where] = part
            turned[where, :columns] = part.T
    place = {(r, c): (u, v) for r, c, u, v in folded(hid // FOLD)}
    per = BLOCK // FOLD
    for r in range(hid // BLOCK):
        for c in range(r, hid // BLOCK):
            value = dot3((high_t[at(r, BLOCK), :], low_t[at(r, BLOCK), :]),
                         (high[:, at(c, BLOCK)], low[:, at(c, BLOCK)]))
            for i in range(per):
                for j in range(per):
                    if (r * per + i, c * per + j) in place:
                        u, v = place[r * per + i, c * per + j]
                        packed[at(u, FOLD), at(v, FOLD)] = value[at(i, FOLD), at(j, FOLD)]


def blend_gram(factor, momentum, grads):
    columns, hid = momentum.shape
    padded = -(-columns // LANES) * LANES
    vmem = pl.BlockSpec(memory_space=pltpu.VMEM)
    return pl.pallas_call(
        blend_gram_kernel,
        in_specs=[vmem] * (2 + STREAMS),
        out_specs=[vmem] * 3,
        out_shape=[
            jax.ShapeDtypeStruct((columns, hid), f32),
            jax.ShapeDtypeStruct((columns, hid), f32),
            jax.ShapeDtypeStruct((hid // 2, hid + FOLD), f32),
        ],
        scratch_shapes=[pltpu.VMEM((padded, hid), bf16)] * 2 + [pltpu.VMEM((hid, padded), bf16)] * 2,
        compiler_params=pltpu.CompilerParams(vmem_limit_bytes=28 * MIB),
    )(factor, momentum, *grads)


def chain_kernel(scale, count, starts, blend, *refs):
    pieces = refs[:count]
    update, packed, gram, ah, al, ph, pll, th, tl, xh, xl, yh, yl, x32, y32 = refs[count:]
    columns, hid = blend.shape
    for k, part in enumerate(pieces):
        packed[pl.ds(pl.multiple_of(starts[k], 8), part.shape[0]), :] = part[...]
    parts = hid // FOLD
    blocks = hid // BLOCK
    pairs = [(r, c) for c in range(blocks) for r in range(c + 1)]
    per = BLOCK // FOLD
    place = {(r, c): (u, v) for r, c, u, v in folded(parts)}
    row = lax.broadcasted_iota(jnp.int32, (BLOCK, BLOCK), 0)
    eye = (row == lax.broadcasted_iota(jnp.int32, (BLOCK, BLOCK), 1)).astype(f32)

    def piece(r, c):
        u, v = place[r, c]
        return packed[at(u, FOLD), at(v, FOLD)]

    small = eye[:FOLD, :FOLD]
    diagonal = sum(piece(r, r) * small for r in range(parts))
    trace = jnp.sum(jnp.sum(diagonal, axis=1, keepdims=True), axis=0, keepdims=True)
    inverse = 1.0 / (jnp.sqrt(trace) + 1e-07)
    inverse_sq = inverse * inverse

    def store(pair, r, c, value):
        for target, part in zip(pair, split(value)):
            target[at(r, BLOCK), at(c, BLOCK)] = part
            if r != c:
                target[at(c, BLOCK), at(r, BLOCK)] = part.T

    def symmetric(left, right, r, c):
        return dot3(tuple(m[at(r, BLOCK), :] for m in left), tuple(m[:, at(c, BLOCK)] for m in right))

    def apply(left, right, c):
        return dot3(tuple(m[...] for m in left), tuple(m[:, at(c, BLOCK)] for m in right))

    a, p, t = (ah, al), (ph, pll), (th, tl)
    x, y = (xh, xl), (yh, yl)

    for r, c in pairs:
        rows = []
        for i in range(per):
            line = []
            for j in range(per):
                u, v = r * per + i, c * per + j
                line.append(piece(u, v) if u <= v else piece(v, u).T)
            rows.append(jnp.concatenate(line, axis=1))
        value = jnp.concatenate(rows, axis=0) * inverse_sq
        gram[at(r, BLOCK), at(c, BLOCK)] = value
        store(a, r, c, value)
    for r in range(blocks):
        for target, part in zip(x, split(blend[:, at(r, BLOCK)] * inverse)):
            target[:, at(r, BLOCK)] = part

    for number in range(ITERS - 1):
        for r, c in pairs:
            value = third_coef * symmetric(a, a, r, c) + second_coef * gram[at(r, BLOCK), at(c, BLOCK)]
            store(p, r, c, value + first_coef * eye if r == c else value)
        for r in range(blocks):
            value = apply(x, p, r)
            if number == ITERS - 2:
                x32[:, at(r, BLOCK)] = value
            for target, part in zip(y, split(value)):
                target[:, at(r, BLOCK)] = part
        x, y = y, x
        for r, c in pairs:
            store(t, r, c, symmetric(a, p, r, c))
        for r, c in pairs:
            value = symmetric(t, p, r, c)
            store(a, r, c, value)
            if number < ITERS - 2:
                gram[at(r, BLOCK), at(c, BLOCK)] = value
    for r in range(blocks):
        value = apply(x, a, r)
        y32[:, at(r, BLOCK)] = value
        for target, part in zip(y, split(value)):
            target[:, at(r, BLOCK)] = part
    for r in range(blocks):
        where = at(r, BLOCK)
        value = first_coef * x32[:, where] + second_coef * y32[:, where] + third_coef * apply(y, a, r)
        update[:, where] = value * scale


def chain(pieces, starts, blend, scale):
    columns, hid = blend.shape
    vmem = pl.BlockSpec(memory_space=pltpu.VMEM)
    square, slab = pltpu.VMEM((hid, hid), bf16), pltpu.VMEM((columns, hid), bf16)
    return pl.pallas_call(
        functools.partial(chain_kernel, scale, len(pieces)),
        in_specs=[pl.BlockSpec(memory_space=pltpu.SMEM)] + [vmem] * (1 + len(pieces)),
        out_specs=vmem,
        out_shape=jax.ShapeDtypeStruct((columns, hid), f32),
        scratch_shapes=[pltpu.VMEM((hid // 2, hid + FOLD), f32), pltpu.VMEM((hid, hid), f32)]
        + [square] * 6 + [slab] * 4 + [pltpu.VMEM((columns, hid), f32)] * 2,
        compiler_params=pltpu.CompilerParams(vmem_limit_bytes=48 * MIB),
    )(starts, blend, *pieces)


def body(local_grads, momentum):
    hid, wid = local_grads.shape[2:]
    ring = Ring("dp")
    rows = hid // STREAMS
    ways = [1 if k % 2 == 0 else -1 for k in range(STREAMS)]
    terms, firsts = zip(*[
        transposed(local_grads, ring.owner(-way), ring.size, k, rows) for k, way in enumerate(ways)
    ])
    grads = ring_sum_scatter(ring, ways, firsts, terms)
    total_sq = jnp.full((8, LANES), sum(jnp.sum(part * part) for part in grads))
    for line in (*two_lines("dp"), Line("expert", lax.axis_size("expert"), 1)):
        total_sq = line.sum(total_sq)
    count = hid * wid * lax.axis_size("expert")
    factor = jnp.minimum(1.0, 1.0 / jnp.sqrt(total_sq / count + 1e-06))
    new_momentum, blend, packed = blend_gram(factor, momentum[0].T, grads)
    pieces, starts = all_sum(packed, "dp")
    update = chain(pieces, starts, blend, 0.2 * math.sqrt(max(hid, wid)))
    return (new_momentum.T[None], update.T[None])


def solution(mesh):
    return jax.shard_map(
        body,
        mesh=mesh,
        in_specs=(P("expert", "dp", None, None), P("expert", None, "dp")),
        out_specs=(P("expert", None, "dp"), P("expert", None, "dp")),
        check_vma=False,
    )
```

```python
import functools
import math

import jax
import jax.numpy as jnp
from jax import lax
from jax.experimental import pallas as pl
from jax.experimental.pallas import tpu as pltpu
from jax.sharding import PartitionSpec as P

ITERS = 3
STREAMS = 4
FOLD = 128
PERMUTED = 8
BLOCK = 256
LANES = 128
MIB = 2**20

first_coef = 3.4445
second_coef = -4.775
third_coef = 2.0315
momentum_decay = 0.95
f32 = jnp.float32
bf16 = jnp.bfloat16


def ring_order(size):
    return list(range(0, size, 2)) + list(range(1, size, 2))[::-1]


def ring_owner(axis, offset):
    size, me = lax.axis_size(axis), lax.axis_index(axis)
    half = lax.div(me, 2)
    position = jnp.where(lax.rem(me, 2) == 0, half, size - 1 - half)
    place = lax.rem(position + offset + size, size)
    return jnp.where(place < (size + 1) // 2, 2 * place, 2 * (size - 1 - place) + 1)


def ring_send(value, axis, way):
    size = lax.axis_size(axis)
    order = ring_order(size)
    return lax.ppermute(value, axis, [(order[p], order[(p + way) % size]) for p in range(size)])


def ring_sum_scatter(axis, ways, firsts, terms):
    held = list(firsts)
    for step in range(lax.axis_size(axis) - 1):
        for k, way in enumerate(ways):
            held[k] = ring_send(held[k], axis, way) + terms[k][step].astype(f32)
    return held


class Line:
    def __init__(self, axis, size, stride):
        self.axis, self.size, self.stride = axis, size, stride

    def digit(self, shift=0):
        own = lax.rem(lax.div(lax.axis_index(self.axis), self.stride), self.size)
        return lax.rem(own + shift + self.size, self.size)

    def send(self, value, shift):
        pairs = []
        for p in range(lax.axis_size(self.axis)):
            digit = p // self.stride % self.size
            pairs.append((p, p + ((digit + shift) % self.size - digit) * self.stride))
        return lax.ppermute(value, self.axis, pairs)

    def everyone(self, value):
        return [value] + [self.send(value, shift) for shift in range(1, self.size)]

    def sum(self, value):
        return sum(self.everyone(value)[1:], value)

    def sum_scatter(self, parts):
        return sum([self.send(parts[shift], shift) for shift in range(1, self.size)], parts[0])


def two_lines(axis):
    size = lax.axis_size(axis)
    inner = 2 if size % 2 == 0 else 1
    return Line(axis, size // inner, inner), Line(axis, inner, 1)


class Cut:
    def __init__(self, rows, axis):
        self.outer, self.inner = two_lines(axis)
        self.members = self.outer.size * self.inner.size
        unit = rows * PERMUTED // 8 // self.members // 8 * 8
        self.small = max(8, 3 * unit // 8 // 8 * 8)
        self.large = unit - self.small
        self.start = self.members * self.large
        self.end = self.members * unit
        self.rest = rows - self.end

    def pieces(self, back):
        sign = -1 if back else 1
        outer, inner = self.outer, self.inner
        for t in range(inner.size):
            for s in range(outer.size):
                y, z = inner.digit(sign * t), outer.digit(sign * s)
                yield 0, t, s * self.large, (y * outer.size + z) * self.large, self.large
                yield 1, s, t * self.small, self.start + (z * inner.size + y) * self.small, self.small

    def shapes(self, width):
        one = [jax.ShapeDtypeStruct((self.outer.size * self.large, width), f32)] * self.inner.size
        two = [jax.ShapeDtypeStruct((self.inner.size * self.small, width), f32)] * self.outer.size
        rest = [jax.ShapeDtypeStruct((self.rest, width), f32)] * (1 if self.rest else 0)
        return one, two, rest

    def split(self, refs):
        one, two = self.inner.size, self.outer.size
        return refs[:one], refs[one:one + two], refs[one + two:]

    def all_sum(self, parts, axis):
        one, two, rest = self.split(parts)
        outer, inner = self.outer, self.inner
        rest = [lax.psum(part, axis) for part in rest]
        one, two = lax.optimization_barrier((inner.sum_scatter(one), outer.sum_scatter(two)))
        one = [one[at(s, self.large)] for s in range(outer.size)]
        two = [two[at(t, self.small)] for t in range(inner.size)]
        one, two = lax.optimization_barrier((outer.sum_scatter(one), inner.sum_scatter(two)))
        one, two = lax.optimization_barrier((outer.everyone(one), inner.everyone(two)))
        one, two = jnp.concatenate(one, axis=0), jnp.concatenate(two, axis=0)
        return [*inner.everyone(one), *outer.everyone(two), *rest]


def at(block, size):
    return slice(block * size, (block + 1) * size)


def transpose_kernel(axis, way, start, source, terms, first, held, turned, sem):
    steps, columns, rows = terms.shape
    copy = pltpu.make_async_copy(source.at[0, 0, pl.ds(start, rows)], held, sem)
    copy.start()
    copy.wait()
    wid = held.shape[1]
    step = 512
    for c in range(0, wid, step):
        width = min(step, wid - c)
        turned[c:c + width, :] = held[:, c:c + width].T

    def owned(offset):
        return turned[pl.ds(pl.multiple_of(ring_owner(axis, offset) * columns, 16), columns), :]

    first[...] = owned(-way).astype(f32)
    for step in range(steps):
        terms[step] = owned(-way * (step + 2))


def transposed(local_grads, axis, way, start, rows):
    wid, size = local_grads.shape[3], lax.axis_size(axis)
    columns = wid // size
    vmem = pl.BlockSpec(memory_space=pltpu.VMEM)
    return pl.pallas_call(
        functools.partial(transpose_kernel, axis, way, start),
        in_specs=[pl.BlockSpec(memory_space=pltpu.HBM)],
        out_specs=[vmem, vmem],
        out_shape=[
            jax.ShapeDtypeStruct((size - 1, columns, rows), local_grads.dtype),
            jax.ShapeDtypeStruct((columns, rows), f32),
        ],
        scratch_shapes=[
            pltpu.VMEM((rows, wid), bf16), pltpu.VMEM((wid, rows), bf16), pltpu.SemaphoreType.DMA,
        ],
        compiler_params=pltpu.CompilerParams(vmem_limit_bytes=14 * MIB),
        cost_estimate=pl.CostEstimate(flops=0, bytes_accessed=4 * rows * wid, transcendentals=0),
    )(local_grads)


def split(value):
    high = value.astype(bf16)
    return high, (value - high.astype(f32)).astype(bf16)


def dot(left, right, contract):
    return lax.dot_general(left, right, ((contract[:1], contract[1:]), ((), ())), preferred_element_type=f32)


def dot3(left, right, contract=(1, 0)):
    (lh, ll), (rh, rl) = left, right
    return dot(lh, rh, contract) + (dot(lh, rl, contract) + dot(ll, rh, contract))


def folded(parts):
    for r in range(parts):
        for c in range(r, parts):
            if r < parts // 2:
                yield r, c, r, c - r
            else:
                yield r, c, parts - 1 - r, parts + 1 - (parts - c)


def blend_gram_kernel(cut, count, squares, momentum, *refs):
    grads = refs[:STREAMS]
    new_momentum, blend, *parts, packed, high, low, high_t, low_t = refs[STREAMS:]
    columns, hid = blend.shape
    total_sq = jnp.sum(jnp.sum(squares[...], axis=1, keepdims=True), axis=0, keepdims=True)
    scale = jnp.minimum(1.0, 1.0 / jnp.sqrt(total_sq / count + 1e-06))
    rows = hid // STREAMS
    if high.shape[0] > columns:
        for target in (high, low):
            target[columns:, :] = jnp.zeros((high.shape[0] - columns, hid), bf16)
        for target in (high_t, low_t):
            target[:, columns:] = jnp.zeros((hid, high.shape[0] - columns), bf16)
    for k in range(STREAMS):
        where = at(k, rows)
        clipped = scale * grads[k][...]
        moved = momentum_decay * momentum[:, where] + clipped
        mixed = clipped + momentum_decay * moved
        new_momentum[:, where] = moved
        blend[:, where] = mixed
        for target, turned, part in zip((high, low), (high_t, low_t), split(mixed)):
            target[:columns, where] = part
            turned[where, :columns] = part.T
    place = {(r, c): (u, v) for r, c, u, v in folded(hid // FOLD)}
    per = BLOCK // FOLD
    for r in range(hid // BLOCK):
        for c in range(r, hid // BLOCK):
            value = dot3((high_t[at(r, BLOCK), :], low_t[at(r, BLOCK), :]),
                         (high[:, at(c, BLOCK)], low[:, at(c, BLOCK)]))
            for i in range(per):
                for j in range(per):
                    if (r * per + i, c * per + j) in place:
                        u, v = place[r * per + i, c * per + j]
                        packed[at(u, FOLD), at(v, FOLD)] = value[at(i, FOLD), at(j, FOLD)]
    *sets, rest = cut.split(parts)
    for which, slot, row, whole, rows in cut.pieces(False):
        sets[which][slot][row:row + rows, :] = packed[pl.ds(pl.multiple_of(whole, 8), rows), :]
    for part in rest:
        part[...] = packed[cut.end:, :]


def blend_gram(cut, count, squares, momentum, grads):
    columns, hid = momentum.shape
    one, two, rest = cut.shapes(hid + FOLD)
    padded = -(-columns // LANES) * LANES
    vmem = pl.BlockSpec(memory_space=pltpu.VMEM)
    return pl.pallas_call(
        functools.partial(blend_gram_kernel, cut, count),
        in_specs=[vmem] * (2 + STREAMS),
        out_specs=[vmem] * (2 + len(one + two + rest)),
        out_shape=[
            jax.ShapeDtypeStruct((columns, hid), f32),
            jax.ShapeDtypeStruct((columns, hid), f32),
            *one, *two, *rest,
        ],
        scratch_shapes=[pltpu.VMEM((hid // 2, hid + FOLD), f32)] + [pltpu.VMEM((padded, hid), bf16)] * 2
        + [pltpu.VMEM((hid, padded), bf16)] * 2,
        compiler_params=pltpu.CompilerParams(vmem_limit_bytes=30 * MIB),
    )(squares, momentum, *grads)


def chain_kernel(scale, cut, count, blend, *refs):
    pieces = refs[:count]
    update, packed, gram, ah, al, ph, pll, th, tl, xh, xl, yh, yl, x32, y32 = refs[count:]
    columns, hid = blend.shape
    *sets, rest = cut.split(pieces)
    for which, slot, row, whole, rows in cut.pieces(True):
        packed[pl.ds(pl.multiple_of(whole, 8), rows), :] = sets[which][slot][row:row + rows, :]
    for part in rest:
        packed[cut.end:, :] = part[...]
    parts = hid // FOLD
    blocks = hid // BLOCK
    pairs = [(r, c) for c in range(blocks) for r in range(c + 1)]
    per = BLOCK // FOLD
    place = {(r, c): (u, v) for r, c, u, v in folded(parts)}
    row = lax.broadcasted_iota(jnp.int32, (BLOCK, BLOCK), 0)
    eye = (row == lax.broadcasted_iota(jnp.int32, (BLOCK, BLOCK), 1)).astype(f32)

    def piece(r, c):
        u, v = place[r, c]
        return packed[at(u, FOLD), at(v, FOLD)]

    small = eye[:FOLD, :FOLD]
    diagonal = sum(piece(r, r) * small for r in range(parts))
    trace = jnp.sum(jnp.sum(diagonal, axis=1, keepdims=True), axis=0, keepdims=True)
    inverse = 1.0 / (jnp.sqrt(trace) + 1e-07)
    inverse_sq = inverse * inverse

    def store(pair, r, c, value):
        for target, part in zip(pair, split(value)):
            target[at(r, BLOCK), at(c, BLOCK)] = part
            if r != c:
                target[at(c, BLOCK), at(r, BLOCK)] = part.T

    def symmetric(left, right):
        for c in range(blocks):
            panel = dot3(tuple(m[:(c + 1) * BLOCK, :] for m in left), tuple(m[:, at(c, BLOCK)] for m in right))
            for r in range(c + 1):
                yield r, c, panel[at(r, BLOCK), :]

    def apply(left, right, c):
        return dot3(tuple(m[...] for m in left), tuple(m[:, at(c, BLOCK)] for m in right))

    a, p, t = (ah, al), (ph, pll), (th, tl)
    x, y = (xh, xl), (yh, yl)

    for r, c in pairs:
        rows = []
        for i in range(per):
            line = []
            for j in range(per):
                u, v = r * per + i, c * per + j
                line.append(piece(u, v) if u <= v else piece(v, u).T)
            rows.append(jnp.concatenate(line, axis=1))
        value = jnp.concatenate(rows, axis=0) * inverse_sq
        gram[at(r, BLOCK), at(c, BLOCK)] = value
        store(a, r, c, value)
    for r in range(blocks):
        for target, part in zip(x, split(blend[:, at(r, BLOCK)] * inverse)):
            target[:, at(r, BLOCK)] = part

    for number in range(ITERS - 1):
        for r, c, value in symmetric(a, a):
            value = third_coef * value + second_coef * gram[at(r, BLOCK), at(c, BLOCK)]
            store(p, r, c, value + first_coef * eye if r == c else value)
        for r in range(blocks):
            value = apply(x, p, r)
            if number == ITERS - 2:
                x32[:, at(r, BLOCK)] = value
            for target, part in zip(y, split(value)):
                target[:, at(r, BLOCK)] = part
        x, y = y, x
        for r, c, value in symmetric(a, p):
            store(t, r, c, value)
        for r, c, value in symmetric(t, p):
            store(a, r, c, value)
            if number < ITERS - 2:
                gram[at(r, BLOCK), at(c, BLOCK)] = value
    for r in range(blocks):
        value = apply(x, a, r)
        y32[:, at(r, BLOCK)] = value
        for target, part in zip(y, split(value)):
            target[:, at(r, BLOCK)] = part
    for r in range(blocks):
        where = at(r, BLOCK)
        value = first_coef * x32[:, where] + second_coef * y32[:, where] + third_coef * apply(y, a, r)
        update[:, where] = value * scale


def chain(cut, pieces, blend, scale):
    columns, hid = blend.shape
    vmem = pl.BlockSpec(memory_space=pltpu.VMEM)
    square, slab = pltpu.VMEM((hid, hid), bf16), pltpu.VMEM((columns, hid), bf16)
    return pl.pallas_call(
        functools.partial(chain_kernel, scale, cut, len(pieces)),
        in_specs=[vmem] * (1 + len(pieces)),
        out_specs=vmem,
        out_shape=jax.ShapeDtypeStruct((columns, hid), f32),
        scratch_shapes=[pltpu.VMEM((hid // 2, hid + FOLD), f32), pltpu.VMEM((hid, hid), f32)]
        + [square] * 6 + [slab] * 4 + [pltpu.VMEM((columns, hid), f32)] * 2,
        compiler_params=pltpu.CompilerParams(vmem_limit_bytes=48 * MIB),
    )(blend, *pieces)


def body(local_grads, momentum):
    hid, wid = local_grads.shape[2:]
    rows = hid // STREAMS
    ways = [1 if k % 2 == 0 else -1 for k in range(STREAMS)]
    source = pltpu.with_memory_space_constraint(local_grads, pltpu.HBM)
    terms, firsts = zip(*[transposed(source, "dp", way, k * rows, rows) for k, way in enumerate(ways)])
    grads = ring_sum_scatter("dp", ways, firsts, terms)
    squares = sum(jnp.sum((part * part).reshape(-1, 8, rows), axis=0) for part in grads)
    for line in (*two_lines("dp"), Line("expert", lax.axis_size("expert"), 1)):
        squares = line.sum(squares)
    cut = Cut(hid // 2, "dp")
    count = hid * wid * lax.axis_size("expert")
    new_momentum, blend, *parts = blend_gram(cut, count, squares, momentum[0].T, grads)
    pieces = cut.all_sum(parts, "dp")
    update = chain(cut, pieces, blend, 0.2 * math.sqrt(max(hid, wid)))
    return (new_momentum.T[None], update.T[None])


def solution(mesh):
    return jax.shard_map(
        body,
        mesh=mesh,
        in_specs=(P("expert", "dp", None, None), P("expert", None, "dp")),
        out_specs=(P("expert", None, "dp"), P("expert", None, "dp")),
        check_vma=False,
    )
```

```python
import functools
import math

import jax
import jax.numpy as jnp
from jax import lax
from jax.experimental import pallas as pl
from jax.experimental.pallas import tpu as pltpu
from jax.sharding import PartitionSpec as P

ITERS = 3
STREAMS = 4
FOLD = 128
PERMUTED = 8
BLOCK = 256
LANES = 128
MIB = 2**20

first_coef = 3.4445
second_coef = -4.775
third_coef = 2.0315
momentum_decay = 0.95
f32 = jnp.float32
bf16 = jnp.bfloat16


def ring_order(size):
    return list(range(0, size, 2)) + list(range(1, size, 2))[::-1]


def ring_owner(axis, offset):
    size, me = lax.axis_size(axis), lax.axis_index(axis)
    half = lax.div(me, 2)
    position = jnp.where(lax.rem(me, 2) == 0, half, size - 1 - half)
    place = lax.rem(position + offset + size, size)
    return jnp.where(place < (size + 1) // 2, 2 * place, 2 * (size - 1 - place) + 1)


def ring_send(value, axis, way):
    size = lax.axis_size(axis)
    order = ring_order(size)
    return lax.ppermute(value, axis, [(order[p], order[(p + way) % size]) for p in range(size)])


def ring_sum_scatter(axis, ways, firsts, terms):
    held = list(firsts)
    for step in range(lax.axis_size(axis) - 1):
        for k, way in enumerate(ways):
            held[k] = ring_send(held[k], axis, way) + terms[k][step].astype(f32)
    return held


class Line:
    def __init__(self, axis, size, stride):
        self.axis, self.size, self.stride = axis, size, stride

    def digit(self, shift=0):
        own = lax.rem(lax.div(lax.axis_index(self.axis), self.stride), self.size)
        return lax.rem(own + shift + self.size, self.size)

    def send(self, value, shift):
        pairs = []
        for p in range(lax.axis_size(self.axis)):
            digit = p // self.stride % self.size
            pairs.append((p, p + ((digit + shift) % self.size - digit) * self.stride))
        return lax.ppermute(value, self.axis, pairs)

    def everyone(self, value):
        return [value] + [self.send(value, shift) for shift in range(1, self.size)]

    def sum(self, value):
        return sum(self.everyone(value)[1:], value)

    def sum_scatter(self, parts):
        return sum([self.send(parts[shift], shift) for shift in range(1, self.size)], parts[0])


def two_lines(axis):
    size = lax.axis_size(axis)
    inner = 2 if size % 2 == 0 else 1
    return Line(axis, size // inner, inner), Line(axis, inner, 1)


class Cut:
    def __init__(self, rows, axis):
        self.outer, self.inner = two_lines(axis)
        self.members = self.outer.size * self.inner.size
        unit = rows * PERMUTED // 8 // self.members // 8 * 8
        self.small = max(8, 3 * unit // 8 // 8 * 8)
        self.large = unit - self.small
        self.start = self.members * self.large
        self.end = self.members * unit
        self.rest = rows - self.end

    def pieces(self, back):
        sign = -1 if back else 1
        outer, inner = self.outer, self.inner
        for t in range(inner.size):
            for s in range(outer.size):
                y, z = inner.digit(sign * t), outer.digit(sign * s)
                yield 0, t, s * self.large, (y * outer.size + z) * self.large, self.large
                yield 1, s, t * self.small, self.start + (z * inner.size + y) * self.small, self.small

    def shapes(self, width):
        one = [jax.ShapeDtypeStruct((self.outer.size * self.large, width), f32)] * self.inner.size
        two = [jax.ShapeDtypeStruct((self.inner.size * self.small, width), f32)] * self.outer.size
        rest = [jax.ShapeDtypeStruct((self.rest, width), f32)] * (1 if self.rest else 0)
        return one, two, rest

    def split(self, refs):
        one, two = self.inner.size, self.outer.size
        return refs[:one], refs[one:one + two], refs[one + two:]

    def all_sum(self, parts, axis):
        one, two, rest = self.split(parts)
        outer, inner = self.outer, self.inner
        rest = [lax.psum(part, axis) for part in rest]
        one, two = lax.optimization_barrier((inner.sum_scatter(one), outer.sum_scatter(two)))
        one = [one[at(s, self.large)] for s in range(outer.size)]
        two = [two[at(t, self.small)] for t in range(inner.size)]
        one, two = lax.optimization_barrier((outer.sum_scatter(one), inner.sum_scatter(two)))
        one, two = lax.optimization_barrier((outer.everyone(one), inner.everyone(two)))
        one, two = jnp.concatenate(one, axis=0), jnp.concatenate(two, axis=0)
        return [*inner.everyone(one), *outer.everyone(two), *rest]


def at(block, size):
    return slice(block * size, (block + 1) * size)


def window(wid, columns):
    spare = LANES - math.gcd(columns, LANES)
    return min(wid, -(-(columns + spare) // LANES) * LANES)


def first_kernel(axis, ways, source, *refs):
    firsts, (held, turned, sems) = refs[:len(ways)], refs[len(ways):]
    columns, rows = firsts[0].shape
    wid, width = source.shape[3], held.shape[2]
    copies, skips = [], []
    for k, way in enumerate(ways):
        begin = ring_owner(axis, -way) * columns
        aligned = pl.multiple_of(jnp.minimum(lax.div(begin, LANES) * LANES, wid - width), LANES)
        skips.append(pl.multiple_of(begin - aligned, math.gcd(columns, LANES)))
        copies.append(pltpu.make_async_copy(
            source.at[0, 0, pl.ds(k * rows, rows), pl.ds(aligned, width)], held.at[k], sems.at[k]
        ))
    for copy in copies:
        copy.start()
    for k, first in enumerate(firsts):
        copies[k].wait()
        turned[...] = held[k].astype(f32).T
        first[...] = turned[pl.ds(skips[k], columns), :]


def first_messages(local_grads, axis, ways, rows):
    wid, size = local_grads.shape[3], lax.axis_size(axis)
    columns = wid // size
    width = window(wid, columns)
    return pl.pallas_call(
        functools.partial(first_kernel, axis, ways),
        in_specs=[pl.BlockSpec(memory_space=pltpu.HBM)],
        out_specs=[pl.BlockSpec(memory_space=pltpu.VMEM)] * len(ways),
        out_shape=[jax.ShapeDtypeStruct((columns, rows), f32)] * len(ways),
        scratch_shapes=[
            pltpu.VMEM((len(ways), rows, width), bf16), pltpu.VMEM((width, rows), f32),
            pltpu.SemaphoreType.DMA((len(ways),)),
        ],
        compiler_params=pltpu.CompilerParams(vmem_limit_bytes=12 * MIB),
        cost_estimate=pl.CostEstimate(flops=0, bytes_accessed=6 * len(ways) * rows * columns, transcendentals=0),
    )(local_grads)


def transpose_kernel(axis, way, start, source, terms, held, turned, sem):
    steps, columns, rows = terms.shape
    copy = pltpu.make_async_copy(source.at[0, 0, pl.ds(start, rows)], held, sem)
    copy.start()
    copy.wait()
    wid = held.shape[1]
    step = 512
    for c in range(0, wid, step):
        width = min(step, wid - c)
        turned[c:c + width, :] = held[:, c:c + width].T
    for step in range(steps):
        owner = ring_owner(axis, -way * (step + 2))
        terms[step] = turned[pl.ds(pl.multiple_of(owner * columns, 16), columns), :]


def transposed(local_grads, axis, way, start, rows):
    wid, size = local_grads.shape[3], lax.axis_size(axis)
    columns = wid // size
    return pl.pallas_call(
        functools.partial(transpose_kernel, axis, way, start),
        in_specs=[pl.BlockSpec(memory_space=pltpu.HBM)],
        out_specs=pl.BlockSpec(memory_space=pltpu.VMEM),
        out_shape=jax.ShapeDtypeStruct((size - 1, columns, rows), local_grads.dtype),
        scratch_shapes=[
            pltpu.VMEM((rows, wid), bf16), pltpu.VMEM((wid, rows), bf16), pltpu.SemaphoreType.DMA,
        ],
        compiler_params=pltpu.CompilerParams(vmem_limit_bytes=14 * MIB),
        cost_estimate=pl.CostEstimate(flops=0, bytes_accessed=4 * rows * wid, transcendentals=0),
    )(local_grads)


def split(value):
    high = value.astype(bf16)
    return high, (value - high.astype(f32)).astype(bf16)


def dot(left, right, contract):
    return lax.dot_general(left, right, ((contract[:1], contract[1:]), ((), ())), preferred_element_type=f32)


def dot3(left, right, contract=(1, 0)):
    (lh, ll), (rh, rl) = left, right
    return dot(lh, rh, contract) + (dot(lh, rl, contract) + dot(ll, rh, contract))


def folded(parts):
    for r in range(parts):
        for c in range(r, parts):
            if r < parts // 2:
                yield r, c, r, c - r
            else:
                yield r, c, parts - 1 - r, parts + 1 - (parts - c)


def blend_gram_kernel(cut, count, squares, momentum, *refs):
    grads = refs[:STREAMS]
    new_momentum, xh, xl, *parts, packed, high, low, high_t, low_t = refs[STREAMS:]
    columns, hid = xh.shape
    total_sq = jnp.sum(jnp.sum(squares[...], axis=1, keepdims=True), axis=0, keepdims=True)
    scale = jnp.minimum(1.0, 1.0 / jnp.sqrt(total_sq / count + 1e-06))
    rows = hid // STREAMS
    if high.shape[0] > columns:
        for target in (high, low):
            target[columns:, :] = jnp.zeros((high.shape[0] - columns, hid), bf16)
        for target in (high_t, low_t):
            target[:, columns:] = jnp.zeros((hid, high.shape[0] - columns), bf16)
    for k in range(STREAMS):
        where = at(k, rows)
        clipped = scale * grads[k][...]
        moved = momentum_decay * momentum[:, where] + clipped
        mixed = clipped + momentum_decay * moved
        new_momentum[:, where] = moved
        for given, target, turned, part in zip((xh, xl), (high, low), (high_t, low_t), split(mixed)):
            given[:, where] = part
            target[:columns, where] = part
            turned[where, :columns] = part.T
    place = {(r, c): (u, v) for r, c, u, v in folded(hid // FOLD)}
    per = BLOCK // FOLD
    for r in range(hid // BLOCK):
        for c in range(r, hid // BLOCK):
            value = dot3((high_t[at(r, BLOCK), :], low_t[at(r, BLOCK), :]),
                         (high[:, at(c, BLOCK)], low[:, at(c, BLOCK)]))
            for i in range(per):
                for j in range(per):
                    if (r * per + i, c * per + j) in place:
                        u, v = place[r * per + i, c * per + j]
                        packed[at(u, FOLD), at(v, FOLD)] = value[at(i, FOLD), at(j, FOLD)]
    *sets, rest = cut.split(parts)
    for which, slot, row, whole, rows in cut.pieces(False):
        sets[which][slot][row:row + rows, :] = packed[pl.ds(pl.multiple_of(whole, 8), rows), :]
    for part in rest:
        part[...] = packed[cut.end:, :]


def blend_gram(cut, count, squares, momentum, grads):
    columns, hid = momentum.shape
    one, two, rest = cut.shapes(hid + FOLD)
    padded = -(-columns // LANES) * LANES
    vmem = pl.BlockSpec(memory_space=pltpu.VMEM)
    return pl.pallas_call(
        functools.partial(blend_gram_kernel, cut, count),
        in_specs=[vmem] * (2 + STREAMS),
        out_specs=[vmem] * (3 + len(one + two + rest)),
        out_shape=[
            jax.ShapeDtypeStruct((columns, hid), f32),
            jax.ShapeDtypeStruct((columns, hid), bf16),
            jax.ShapeDtypeStruct((columns, hid), bf16),
            *one, *two, *rest,
        ],
        scratch_shapes=[pltpu.VMEM((hid // 2, hid + FOLD), f32)] + [pltpu.VMEM((padded, hid), bf16)] * 2
        + [pltpu.VMEM((hid, padded), bf16)] * 2,
        compiler_params=pltpu.CompilerParams(vmem_limit_bytes=30 * MIB),
    )(squares, momentum, *grads)


def chain_kernel(scale, cut, count, given_high, given_low, *refs):
    pieces = refs[:count]
    update, packed, gram, al, ar, pr, tl, xl, yl, x32, y32 = refs[count:]
    columns, hid = update.shape
    *sets, rest = cut.split(pieces)
    for which, slot, row, whole, rows in cut.pieces(True):
        packed[pl.ds(pl.multiple_of(whole, 8), rows), :] = sets[which][slot][row:row + rows, :]
    for part in rest:
        packed[cut.end:, :] = part[...]
    parts = hid // FOLD
    blocks = hid // BLOCK
    pairs = [(r, c) for c in range(blocks) for r in range(c + 1)]
    per = BLOCK // FOLD
    place = {(r, c): (u, v) for r, c, u, v in folded(parts)}
    row = lax.broadcasted_iota(jnp.int32, (BLOCK, BLOCK), 0)
    eye = (row == lax.broadcasted_iota(jnp.int32, (BLOCK, BLOCK), 1)).astype(f32)

    def piece(r, c):
        u, v = place[r, c]
        return packed[at(u, FOLD), at(v, FOLD)]

    small = eye[:FOLD, :FOLD]
    diagonal = sum(piece(r, r) * small for r in range(parts))
    trace = jnp.sum(jnp.sum(diagonal, axis=1, keepdims=True), axis=0, keepdims=True)
    inverse = 1.0 / (jnp.sqrt(trace) + 1e-07)
    inverse_sq = inverse * inverse

    def store_left(target, rows, c, high, low):
        for k, part in enumerate((high, low, high)):
            target[rows, k * hid + c * BLOCK:k * hid + (c + 1) * BLOCK] = part

    def store_right(target, r, c, high, low):
        for k, part in enumerate((high, high, low)):
            target[k * hid + r * BLOCK:k * hid + (r + 1) * BLOCK, at(c, BLOCK)] = part

    def store(left, right, r, c, value):
        high, low = split(value)
        places = [(r, c, high, low)] + ([(c, r, high.T, low.T)] if r != c else [])
        for i, j, first, second in places:
            if left is not None:
                store_left(left, at(i, BLOCK), j, first, second)
            if right is not None:
                store_right(right, i, j, first, second)

    def symmetric(left, right, r, c):
        return dot(left[at(r, BLOCK), :], right[:, at(c, BLOCK)], (1, 0))

    def apply(left, right, c):
        return dot(left[...], right[:, at(c, BLOCK)], (1, 0))

    for r, c in pairs:
        rows = []
        for i in range(per):
            line = []
            for j in range(per):
                u, v = r * per + i, c * per + j
                line.append(piece(u, v) if u <= v else piece(v, u).T)
            rows.append(jnp.concatenate(line, axis=1))
        value = jnp.concatenate(rows, axis=0) * inverse_sq
        gram[at(r, BLOCK), at(c, BLOCK)] = value
        store(al, ar, r, c, value)
    x, y = xl, yl
    for k, part in enumerate((given_high, given_low, given_high)):
        x[:, at(k, hid)] = part[...]

    for number in range(ITERS - 1):
        for r, c in pairs:
            value = third_coef * symmetric(al, ar, r, c) + second_coef * gram[at(r, BLOCK), at(c, BLOCK)]
            store(None, pr, r, c, value + first_coef * eye if r == c else value)
        for c in range(blocks):
            value = apply(x, pr, c)
            if number == ITERS - 2:
                x32[:, at(c, BLOCK)] = value
            store_left(y, slice(None), c, *split(value))
        x, y = y, x
        for r, c in pairs:
            store(tl, None, r, c, symmetric(al, pr, r, c))
        for r, c in pairs:
            value = symmetric(tl, pr, r, c)
            last = number == ITERS - 2
            store(None if last else al, ar, r, c, value)
            if not last:
                gram[at(r, BLOCK), at(c, BLOCK)] = value
    for c in range(blocks):
        value = apply(x, ar, c)
        y32[:, at(c, BLOCK)] = value
        store_left(y, slice(None), c, *split(value))
    factor = inverse * scale
    for c in range(blocks):
        where = at(c, BLOCK)
        value = first_coef * x32[:, where] + second_coef * y32[:, where] + third_coef * apply(y, ar, c)
        update[:, where] = value * factor


def chain(cut, pieces, high, low, scale):
    columns, hid = high.shape
    vmem = pl.BlockSpec(memory_space=pltpu.VMEM)
    left, right = pltpu.VMEM((hid, 3 * hid), bf16), pltpu.VMEM((3 * hid, hid), bf16)
    slab, full = pltpu.VMEM((columns, 3 * hid), bf16), pltpu.VMEM((columns, hid), f32)
    return pl.pallas_call(
        functools.partial(chain_kernel, scale, cut, len(pieces)),
        in_specs=[vmem] * (2 + len(pieces)),
        out_specs=vmem,
        out_shape=jax.ShapeDtypeStruct((columns, hid), f32),
        scratch_shapes=[
            pltpu.VMEM((hid // 2, hid + FOLD), f32), pltpu.VMEM((hid, hid), f32),
            left, right, right, left, slab, slab, full, full,
        ],
        compiler_params=pltpu.CompilerParams(vmem_limit_bytes=46 * MIB),
    )(high, low, *pieces)


def body(local_grads, momentum):
    hid, wid = local_grads.shape[2:]
    rows = hid // STREAMS
    ways = [1 if k % 2 == 0 else -1 for k in range(STREAMS)]
    source = pltpu.with_memory_space_constraint(local_grads, pltpu.HBM)
    firsts = first_messages(source, "dp", ways, rows)
    terms = [transposed(source, "dp", way, k * rows, rows) for k, way in enumerate(ways)]
    grads = ring_sum_scatter("dp", ways, firsts, terms)
    squares = sum(jnp.sum((part * part).reshape(-1, 8, rows), axis=0) for part in grads)
    for line in (*two_lines("dp"), Line("expert", lax.axis_size("expert"), 1)):
        squares = line.sum(squares)
    cut = Cut(hid // 2, "dp")
    count = hid * wid * lax.axis_size("expert")
    new_momentum, high, low, *parts = blend_gram(cut, count, squares, momentum[0].T, grads)
    pieces = cut.all_sum(parts, "dp")
    update = chain(cut, pieces, high, low, 0.2 * math.sqrt(max(hid, wid)))
    return (new_momentum.T[None], update.T[None])


def solution(mesh):
    return jax.shard_map(
        body,
        mesh=mesh,
        in_specs=(P("expert", "dp", None, None), P("expert", None, "dp")),
        out_specs=(P("expert", None, "dp"), P("expert", None, "dp")),
        check_vma=False,
    )
```

```python
import functools
import math

import jax
import jax.numpy as jnp
from jax import lax
from jax.experimental import pallas as pl
from jax.experimental.pallas import tpu as pltpu
from jax.sharding import PartitionSpec as P

ITERS = 3
STREAMS = 4
FOLD = 128
EXTRA = 8
BLOCK = 256
LANES = 128
MIB = 2**20

first_coef = 3.4445
second_coef = -4.775
third_coef = 2.0315
momentum_decay = 0.95
f32 = jnp.float32
bf16 = jnp.bfloat16


def ring_order(size):
    return list(range(0, size, 2)) + list(range(1, size, 2))[::-1]


def ring_owner(axis, offset):
    size, me = lax.axis_size(axis), lax.axis_index(axis)
    half = lax.div(me, 2)
    position = jnp.where(lax.rem(me, 2) == 0, half, size - 1 - half)
    place = lax.rem(position + offset + size, size)
    return jnp.where(place < (size + 1) // 2, 2 * place, 2 * (size - 1 - place) + 1)


def ring_send(value, axis, way):
    size = lax.axis_size(axis)
    order = ring_order(size)
    return lax.ppermute(value, axis, [(order[p], order[(p + way) % size]) for p in range(size)])


def ring_sum_scatter(axis, ways, firsts, terms):
    held = list(firsts)
    for step in range(lax.axis_size(axis) - 1):
        for k, way in enumerate(ways):
            held[k] = ring_send(held[k], axis, way) + terms[k][step].astype(f32)
    return held


class Line:
    def __init__(self, axis, size, stride):
        self.axis, self.size, self.stride = axis, size, stride

    def digit(self, shift=0):
        own = lax.rem(lax.div(lax.axis_index(self.axis), self.stride), self.size)
        return lax.rem(own + shift + self.size, self.size)

    def send(self, value, shift):
        pairs = []
        for p in range(lax.axis_size(self.axis)):
            digit = p // self.stride % self.size
            pairs.append((p, p + ((digit + shift) % self.size - digit) * self.stride))
        return lax.ppermute(value, self.axis, pairs)

    def everyone(self, value):
        return [value] + [self.send(value, shift) for shift in range(1, self.size)]

    def sum(self, value):
        return sum(self.everyone(value)[1:], value)

    def sum_scatter(self, parts):
        return sum([self.send(parts[shift], shift) for shift in range(1, self.size)], parts[0])


def two_lines(axis):
    size = lax.axis_size(axis)
    inner = 2 if size % 2 == 0 else 1
    return Line(axis, size // inner, inner), Line(axis, inner, 1)


class Cut:
    def __init__(self, rows, axis):
        self.outer, self.inner = two_lines(axis)
        unit = rows // (self.outer.size * self.inner.size)
        self.small = max(8, unit // 24 * 8)
        self.large = unit - self.small
        self.start = self.outer.size * self.inner.size * self.large

    def pieces(self, back):
        sign = -1 if back else 1
        outer, inner = self.outer, self.inner
        step = self.large + (EXTRA if back else 0)
        for t in range(inner.size):
            for s in range(outer.size):
                y, z = inner.digit(sign * t), outer.digit(sign * s)
                yield 0, t, s * step, (y * outer.size + z) * self.large, self.large
                yield 1, s, t * self.small, self.start + (z * inner.size + y) * self.small, self.small

    def shapes(self):
        one = jax.ShapeDtypeStruct((self.outer.size * self.large + EXTRA, LANES), f32)
        two = jax.ShapeDtypeStruct((self.inner.size * self.small, LANES), f32)
        return [one] * self.inner.size + [two] * self.outer.size

    def split(self, refs):
        return refs[:self.inner.size], refs[self.inner.size:]

    def all_sum(self, parts):
        one, two = self.split(parts)
        outer, inner = self.outer, self.inner
        one, two = lax.optimization_barrier((inner.sum_scatter(one), outer.sum_scatter(two)))
        one = [jnp.concatenate([one[at(s, self.large)], one[-EXTRA:]]) for s in range(outer.size)]
        two = [two[at(t, self.small)] for t in range(inner.size)]
        one, two = lax.optimization_barrier((outer.sum_scatter(one), inner.sum_scatter(two)))
        one, two = lax.optimization_barrier((outer.everyone(one), inner.everyone(two)))
        one, two = jnp.concatenate(one, axis=0), jnp.concatenate(two, axis=0)
        return [*inner.everyone(one), *outer.everyone(two)]


def at(block, size):
    return slice(block * size, (block + 1) * size)


def window(wid, columns):
    spare = LANES - math.gcd(columns, LANES)
    return min(wid, -(-(columns + spare) // LANES) * LANES)


def first_kernel(axis, ways, source, *refs):
    firsts, (held, turned, sems) = refs[:len(ways)], refs[len(ways):]
    columns, rows = firsts[0].shape
    wid, width = source.shape[3], held.shape[2]
    copies, skips = [], []
    for k, way in enumerate(ways):
        begin = ring_owner(axis, -way) * columns
        aligned = pl.multiple_of(jnp.minimum(lax.div(begin, LANES) * LANES, wid - width), LANES)
        skips.append(pl.multiple_of(begin - aligned, math.gcd(columns, LANES)))
        copies.append(pltpu.make_async_copy(
            source.at[0, 0, pl.ds(k * rows, rows), pl.ds(aligned, width)], held.at[k], sems.at[k]
        ))
    for copy in copies:
        copy.start()
    for k, first in enumerate(firsts):
        copies[k].wait()
        turned[...] = held[k].astype(f32).T
        first[...] = turned[pl.ds(skips[k], columns), :]


def first_messages(local_grads, axis, ways, rows):
    wid, size = local_grads.shape[3], lax.axis_size(axis)
    columns = wid // size
    width = window(wid, columns)
    return pl.pallas_call(
        functools.partial(first_kernel, axis, ways),
        in_specs=[pl.BlockSpec(memory_space=pltpu.HBM)],
        out_specs=[pl.BlockSpec(memory_space=pltpu.VMEM)] * len(ways),
        out_shape=[jax.ShapeDtypeStruct((columns, rows), f32)] * len(ways),
        scratch_shapes=[
            pltpu.VMEM((len(ways), rows, width), bf16), pltpu.VMEM((width, rows), f32),
            pltpu.SemaphoreType.DMA((len(ways),)),
        ],
        compiler_params=pltpu.CompilerParams(vmem_limit_bytes=12 * MIB),
        cost_estimate=pl.CostEstimate(flops=0, bytes_accessed=6 * len(ways) * rows * columns, transcendentals=0),
    )(local_grads)


def transpose_kernel(axis, way, start, source, terms, held, turned, sem):
    steps, columns, rows = terms.shape
    copy = pltpu.make_async_copy(source.at[0, 0, pl.ds(start, rows)], held, sem)
    copy.start()
    copy.wait()
    wid = held.shape[1]
    step = 512
    for c in range(0, wid, step):
        width = min(step, wid - c)
        turned[c:c + width, :] = held[:, c:c + width].T
    for step in range(steps):
        owner = ring_owner(axis, -way * (step + 2))
        terms[step] = turned[pl.ds(pl.multiple_of(owner * columns, 16), columns), :]


def transposed(local_grads, axis, way, start, rows):
    wid, size = local_grads.shape[3], lax.axis_size(axis)
    columns = wid // size
    return pl.pallas_call(
        functools.partial(transpose_kernel, axis, way, start),
        in_specs=[pl.BlockSpec(memory_space=pltpu.HBM)],
        out_specs=pl.BlockSpec(memory_space=pltpu.VMEM),
        out_shape=jax.ShapeDtypeStruct((size - 1, columns, rows), local_grads.dtype),
        scratch_shapes=[
            pltpu.VMEM((rows, wid), bf16), pltpu.VMEM((wid, rows), bf16), pltpu.SemaphoreType.DMA,
        ],
        compiler_params=pltpu.CompilerParams(vmem_limit_bytes=14 * MIB),
        cost_estimate=pl.CostEstimate(flops=0, bytes_accessed=4 * rows * wid, transcendentals=0),
    )(local_grads)


def split(value):
    high = value.astype(bf16)
    return high, (value - high.astype(f32)).astype(bf16)


def dot(left, right, contract):
    return lax.dot_general(left, right, ((contract[:1], contract[1:]), ((), ())), preferred_element_type=f32)


def dot3(left, right, contract=(1, 0)):
    (lh, ll), (rh, rl) = left, right
    return dot(lh, rh, contract) + (dot(lh, rl, contract) + dot(ll, rh, contract))


def block_order(parts):
    place = {}
    for r in range(parts):
        for c in range(r + 1, parts):
            place[r, c] = len(place)
    for p in range(parts // 2):
        place[p, p] = place[parts - 1 - p, parts - 1 - p] = parts * (parts - 1) // 2 + p
    return place


def triangle_masks():
    row = lax.broadcasted_iota(jnp.int32, (FOLD, FOLD), 0)
    column = lax.broadcasted_iota(jnp.int32, (FOLD, FOLD), 1)
    return row <= column, row == column


def blend_gram_kernel(cut, count, squares, momentum, *refs):
    grads = refs[:STREAMS]
    new_momentum, xh, xl, *parts, packed, extra, high, low, high_t, low_t = refs[STREAMS:]
    columns, hid = xh.shape
    sets = cut.split(parts)
    total_sq = jnp.sum(jnp.sum(squares[...], axis=1, keepdims=True), axis=0, keepdims=True)
    scale = jnp.minimum(1.0, 1.0 / jnp.sqrt(total_sq / count + 1e-06))
    rows = hid // STREAMS
    if high.shape[0] > columns:
        for target in (high, low):
            target[columns:, :] = jnp.zeros((high.shape[0] - columns, hid), bf16)
        for target in (high_t, low_t):
            target[:, columns:] = jnp.zeros((hid, high.shape[0] - columns), bf16)
    for k in range(STREAMS):
        where = at(k, rows)
        clipped = scale * grads[k][...]
        moved = momentum_decay * momentum[:, where] + clipped
        mixed = clipped + momentum_decay * moved
        new_momentum[:, where] = moved
        for given, target, turned, part in zip((xh, xl), (high, low), (high_t, low_t), split(mixed)):
            given[:, where] = part
            target[:columns, where] = part
            turned[where, :columns] = part.T
    parts, per = hid // FOLD, BLOCK // FOLD
    place = block_order(parts)
    upper, diagonal = triangle_masks()
    extra[...] = jnp.zeros(extra.shape, f32)
    for r in range(hid // BLOCK):
        for c in range(r, hid // BLOCK):
            value = dot3((high_t[at(r, BLOCK), :], low_t[at(r, BLOCK), :]),
                         (high[:, at(c, BLOCK)], low[:, at(c, BLOCK)]))
            for i in range(per):
                for j in range(per):
                    u, v = r * per + i, c * per + j
                    if u > v:
                        continue
                    block, where = value[at(i, FOLD), at(j, FOLD)], at(place[u, v], FOLD)
                    if u == v and u >= parts // 2:
                        line = parts - 1 - u
                        extra[line:line + 1, :] = jnp.sum(jnp.where(diagonal, block, 0.0), axis=0, keepdims=True)
                        block = jnp.where(upper, packed[where, :], block)
                    packed[where, :] = block
    for which, slot, row, whole, rows in cut.pieces(False):
        sets[which][slot][row:row + rows, :] = packed[pl.ds(pl.multiple_of(whole, 8), rows), :]
    for part in sets[0]:
        part[part.shape[0] - EXTRA:, :] = extra[...]


def blend_gram(cut, count, squares, momentum, grads):
    columns, hid = momentum.shape
    shapes = cut.shapes()
    padded = -(-columns // LANES) * LANES
    vmem = pl.BlockSpec(memory_space=pltpu.VMEM)
    return pl.pallas_call(
        functools.partial(blend_gram_kernel, cut, count),
        in_specs=[vmem] * (2 + STREAMS),
        out_specs=[vmem] * (3 + len(shapes)),
        out_shape=[
            jax.ShapeDtypeStruct((columns, hid), f32),
            jax.ShapeDtypeStruct((columns, hid), bf16),
            jax.ShapeDtypeStruct((columns, hid), bf16),
            *shapes,
        ],
        scratch_shapes=[pltpu.VMEM((hid * hid // 2 // LANES, LANES), f32), pltpu.VMEM((EXTRA, LANES), f32)]
        + [pltpu.VMEM((padded, hid), bf16)] * 2
        + [pltpu.VMEM((hid, padded), bf16)] * 2,
        compiler_params=pltpu.CompilerParams(vmem_limit_bytes=30 * MIB),
    )(squares, momentum, *grads)


def chain_kernel(scale, cut, count, given_high, given_low, *refs):
    pieces = refs[:count]
    update, packed, gram, al, ar, pr, tl, xl, yl, x32, y32 = refs[count:]
    columns, hid = update.shape
    sets = cut.split(pieces)
    for which, slot, row, whole, rows in cut.pieces(True):
        packed[pl.ds(pl.multiple_of(whole, 8), rows), :] = sets[which][slot][row:row + rows, :]
    extra = sets[0][0][cut.large:cut.large + EXTRA, :]
    parts = hid // FOLD
    blocks = hid // BLOCK
    pairs = [(r, c) for c in range(blocks) for r in range(c + 1)]
    per = BLOCK // FOLD
    place = block_order(parts)
    upper, diagonal = triangle_masks()
    row = lax.broadcasted_iota(jnp.int32, (BLOCK, BLOCK), 0)
    eye = (row == lax.broadcasted_iota(jnp.int32, (BLOCK, BLOCK), 1)).astype(f32)

    def piece(r, c):
        value = packed[at(place[min(r, c), max(r, c)], FOLD), :]
        if r > c:
            return value.T
        if r < c:
            return value
        if r < parts // 2:
            return jnp.where(upper, value, value.T)
        line = parts - 1 - r
        return jnp.where(diagonal, extra[line:line + 1, :], jnp.where(upper, value.T, value))

    trace = extra + sum(
        jnp.sum(jnp.where(diagonal, packed[at(place[p, p], FOLD), :], 0.0).reshape(-1, EXTRA, LANES), axis=0)
        for p in range(parts // 2)
    )
    trace = jnp.sum(jnp.sum(trace, axis=1, keepdims=True), axis=0, keepdims=True)
    inverse = 1.0 / (jnp.sqrt(trace) + 1e-07)
    inverse_sq = inverse * inverse

    def store_left(target, rows, c, high, low):
        for k, part in enumerate((high, low, high)):
            target[rows, k * hid + c * BLOCK:k * hid + (c + 1) * BLOCK] = part

    def store_right(target, r, c, high, low):
        for k, part in enumerate((high, high, low)):
            target[k * hid + r * BLOCK:k * hid + (r + 1) * BLOCK, at(c, BLOCK)] = part

    def store(left, right, r, c, value):
        high, low = split(value)
        places = [(r, c, high, low)] + ([(c, r, high.T, low.T)] if r != c else [])
        for i, j, first, second in places:
            if left is not None:
                store_left(left, at(i, BLOCK), j, first, second)
            if right is not None:
                store_right(right, i, j, first, second)

    def symmetric(left, right, r, c):
        return dot(left[at(r, BLOCK), :], right[:, at(c, BLOCK)], (1, 0))

    def apply(left, right, c):
        return dot(left[...], right[:, at(c, BLOCK)], (1, 0))

    for r, c in pairs:
        rows = []
        for i in range(per):
            line = []
            for j in range(per):
                u, v = r * per + i, c * per + j
                line.append(piece(u, v))
            rows.append(jnp.concatenate(line, axis=1))
        value = jnp.concatenate(rows, axis=0) * inverse_sq
        gram[at(r, BLOCK), at(c, BLOCK)] = value
        store(al, ar, r, c, value)
    x, y = xl, yl
    for k, part in enumerate((given_high, given_low, given_high)):
        x[:, at(k, hid)] = part[...]

    for number in range(ITERS - 1):
        for r, c in pairs:
            value = third_coef * symmetric(al, ar, r, c) + second_coef * gram[at(r, BLOCK), at(c, BLOCK)]
            store(None, pr, r, c, value + first_coef * eye if r == c else value)
        for c in range(blocks):
            value = apply(x, pr, c)
            if number == ITERS - 2:
                x32[:, at(c, BLOCK)] = value
            store_left(y, slice(None), c, *split(value))
        x, y = y, x
        for r, c in pairs:
            store(tl, None, r, c, symmetric(al, pr, r, c))
        for r, c in pairs:
            value = symmetric(tl, pr, r, c)
            last = number == ITERS - 2
            store(None if last else al, ar, r, c, value)
            if not last:
                gram[at(r, BLOCK), at(c, BLOCK)] = value
    for c in range(blocks):
        value = apply(x, ar, c)
        y32[:, at(c, BLOCK)] = value
        store_left(y, slice(None), c, *split(value))
    factor = inverse * scale
    for c in range(blocks):
        where = at(c, BLOCK)
        value = first_coef * x32[:, where] + second_coef * y32[:, where] + third_coef * apply(y, ar, c)
        update[:, where] = value * factor


def chain(cut, pieces, high, low, scale):
    columns, hid = high.shape
    vmem = pl.BlockSpec(memory_space=pltpu.VMEM)
    left, right = pltpu.VMEM((hid, 3 * hid), bf16), pltpu.VMEM((3 * hid, hid), bf16)
    slab, full = pltpu.VMEM((columns, 3 * hid), bf16), pltpu.VMEM((columns, hid), f32)
    return pl.pallas_call(
        functools.partial(chain_kernel, scale, cut, len(pieces)),
        in_specs=[vmem] * (2 + len(pieces)),
        out_specs=vmem,
        out_shape=jax.ShapeDtypeStruct((columns, hid), f32),
        scratch_shapes=[
            pltpu.VMEM((hid * hid // 2 // LANES, LANES), f32), pltpu.VMEM((hid, hid), f32),
            left, right, right, left, slab, slab, full, full,
        ],
        compiler_params=pltpu.CompilerParams(vmem_limit_bytes=46 * MIB),
    )(high, low, *pieces)


def body(local_grads, momentum):
    hid, wid = local_grads.shape[2:]
    rows = hid // STREAMS
    ways = [1 if k % 2 == 0 else -1 for k in range(STREAMS)]
    source = pltpu.with_memory_space_constraint(local_grads, pltpu.HBM)
    firsts = first_messages(source, "dp", ways, rows)
    terms = [transposed(source, "dp", way, k * rows, rows) for k, way in enumerate(ways)]
    grads = ring_sum_scatter("dp", ways, firsts, terms)
    squares = sum(jnp.sum((part * part).reshape(-1, 8, rows), axis=0) for part in grads)
    for line in (*two_lines("dp"), Line("expert", lax.axis_size("expert"), 1)):
        squares = line.sum(squares)
    cut = Cut(hid * hid // 2 // LANES, "dp")
    count = hid * wid * lax.axis_size("expert")
    new_momentum, high, low, *parts = blend_gram(cut, count, squares, momentum[0].T, grads)
    pieces = cut.all_sum(parts)
    update = chain(cut, pieces, high, low, 0.2 * math.sqrt(max(hid, wid)))
    return (new_momentum.T[None], update.T[None])


def solution(mesh):
    return jax.shard_map(
        body,
        mesh=mesh,
        in_specs=(P("expert", "dp", None, None), P("expert", None, "dp")),
        out_specs=(P("expert", None, "dp"), P("expert", None, "dp")),
        check_vma=False,
    )
```

```python
import functools
import math

import jax
import jax.numpy as jnp
from jax import lax
from jax.experimental import pallas as pl
from jax.experimental.pallas import tpu as pltpu
from jax.sharding import PartitionSpec as P

ITERS = 3
STREAMS = 4
FOLD = 128
EXTRA = 8
BLOCK = 256
LANES = 128
MIB = 2**20

first_coef = 3.4445
second_coef = -4.775
third_coef = 2.0315
momentum_decay = 0.95
f32 = jnp.float32
bf16 = jnp.bfloat16


def ring_order(size):
    return list(range(0, size, 2)) + list(range(1, size, 2))[::-1]


def ring_owner(axis, offset):
    size, me = lax.axis_size(axis), lax.axis_index(axis)
    half = lax.div(me, 2)
    position = jnp.where(lax.rem(me, 2) == 0, half, size - 1 - half)
    place = lax.rem(position + offset + size, size)
    return jnp.where(place < (size + 1) // 2, 2 * place, 2 * (size - 1 - place) + 1)


def ring_send(value, axis, way):
    size = lax.axis_size(axis)
    order = ring_order(size)
    return lax.ppermute(value, axis, [(order[p], order[(p + way) % size]) for p in range(size)])


def ring_sum_scatter(axis, ways, firsts, terms):
    held = list(firsts)
    for step in range(lax.axis_size(axis) - 1):
        for k, way in enumerate(ways):
            held[k] = ring_send(held[k], axis, way) + terms[k][step].astype(f32)
    return held


class Line:
    def __init__(self, axis, size, stride):
        self.axis, self.size, self.stride = axis, size, stride

    def digit(self, shift=0):
        own = lax.rem(lax.div(lax.axis_index(self.axis), self.stride), self.size)
        return lax.rem(own + shift + self.size, self.size)

    def send(self, value, shift):
        pairs = []
        for p in range(lax.axis_size(self.axis)):
            digit = p // self.stride % self.size
            pairs.append((p, p + ((digit + shift) % self.size - digit) * self.stride))
        return lax.ppermute(value, self.axis, pairs)

    def everyone(self, value):
        return [value] + [self.send(value, shift) for shift in range(1, self.size)]

    def sum(self, value):
        return sum(self.everyone(value)[1:], value)

    def sum_scatter(self, parts):
        return sum([self.send(parts[shift], shift) for shift in range(1, self.size)], parts[0])


def two_lines(axis):
    size = lax.axis_size(axis)
    inner = 2 if size % 2 == 0 else 1
    return Line(axis, size // inner, inner), Line(axis, inner, 1)


class Cut:
    def __init__(self, rows, axis):
        self.outer, self.inner = two_lines(axis)
        unit = rows // (self.outer.size * self.inner.size)
        self.small = max(8, unit // 24 * 8)
        self.large = unit - self.small
        self.start = self.outer.size * self.inner.size * self.large

    def pieces(self, back):
        sign = -1 if back else 1
        outer, inner = self.outer, self.inner
        step = self.large + (EXTRA if back else 0)
        for t in range(inner.size):
            for s in range(outer.size):
                y, z = inner.digit(sign * t), outer.digit(sign * s)
                yield 0, t, s * step, (y * outer.size + z) * self.large, self.large
                yield 1, s, t * self.small, self.start + (z * inner.size + y) * self.small, self.small

    def shapes(self):
        one = jax.ShapeDtypeStruct((self.outer.size * self.large + EXTRA, LANES), f32)
        two = jax.ShapeDtypeStruct((self.inner.size * self.small, LANES), f32)
        return [one] * self.inner.size + [two] * self.outer.size

    def split(self, refs):
        return refs[:self.inner.size], refs[self.inner.size:]

    def all_sum(self, parts):
        one, two = self.split(parts)
        outer, inner = self.outer, self.inner
        one, two = lax.optimization_barrier((inner.sum_scatter(one), outer.sum_scatter(two)))
        one = [jnp.concatenate([one[at(s, self.large)], one[-EXTRA:]]) for s in range(outer.size)]
        two = [two[at(t, self.small)] for t in range(inner.size)]
        one, two = lax.optimization_barrier((outer.sum_scatter(one), inner.sum_scatter(two)))
        one, two = lax.optimization_barrier((outer.everyone(one), inner.everyone(two)))
        one, two = jnp.concatenate(one, axis=0), jnp.concatenate(two, axis=0)
        return [*inner.everyone(one), *outer.everyone(two)]


def at(block, size):
    return slice(block * size, (block + 1) * size)


def window(wid, columns):
    spare = LANES - math.gcd(columns, LANES)
    return min(wid, -(-(columns + spare) // LANES) * LANES)


def first_kernel(axis, ways, source, *refs):
    firsts, (held, turned, sems) = refs[:len(ways)], refs[len(ways):]
    columns, rows = firsts[0].shape
    wid, width = source.shape[3], held.shape[2]
    copies, skips = [], []
    for k, way in enumerate(ways):
        begin = ring_owner(axis, -way) * columns
        aligned = pl.multiple_of(jnp.minimum(lax.div(begin, LANES) * LANES, wid - width), LANES)
        skips.append(pl.multiple_of(begin - aligned, math.gcd(columns, LANES)))
        copies.append(pltpu.make_async_copy(
            source.at[0, 0, pl.ds(k * rows, rows), pl.ds(aligned, width)], held.at[k], sems.at[k]
        ))
    for copy in copies:
        copy.start()
    for k, first in enumerate(firsts):
        copies[k].wait()
        turned[...] = held[k].astype(f32).T
        first[...] = turned[pl.ds(skips[k], columns), :]


def first_messages(local_grads, axis, ways, rows):
    wid, size = local_grads.shape[3], lax.axis_size(axis)
    columns = wid // size
    width = window(wid, columns)
    return pl.pallas_call(
        functools.partial(first_kernel, axis, ways),
        in_specs=[pl.BlockSpec(memory_space=pltpu.HBM)],
        out_specs=[pl.BlockSpec(memory_space=pltpu.VMEM)] * len(ways),
        out_shape=[jax.ShapeDtypeStruct((columns, rows), f32)] * len(ways),
        scratch_shapes=[
            pltpu.VMEM((len(ways), rows, width), bf16), pltpu.VMEM((width, rows), f32),
            pltpu.SemaphoreType.DMA((len(ways),)),
        ],
        compiler_params=pltpu.CompilerParams(vmem_limit_bytes=12 * MIB),
        cost_estimate=pl.CostEstimate(flops=0, bytes_accessed=6 * len(ways) * rows * columns, transcendentals=0),
    )(local_grads)


def transpose_kernel(axis, way, start, source, terms, held, turned, sem):
    steps, columns, rows = terms.shape
    copy = pltpu.make_async_copy(source.at[0, 0, pl.ds(start, rows)], held, sem)
    copy.start()
    copy.wait()
    wid = held.shape[1]
    step = 512
    for c in range(0, wid, step):
        width = min(step, wid - c)
        turned[c:c + width, :] = held[:, c:c + width].T
    for step in range(steps):
        owner = ring_owner(axis, -way * (step + 2))
        terms[step] = turned[pl.ds(pl.multiple_of(owner * columns, 16), columns), :]


def transposed(local_grads, axis, way, start, rows):
    wid, size = local_grads.shape[3], lax.axis_size(axis)
    columns = wid // size
    return pl.pallas_call(
        functools.partial(transpose_kernel, axis, way, start),
        in_specs=[pl.BlockSpec(memory_space=pltpu.HBM)],
        out_specs=pl.BlockSpec(memory_space=pltpu.VMEM),
        out_shape=jax.ShapeDtypeStruct((size - 1, columns, rows), local_grads.dtype),
        scratch_shapes=[
            pltpu.VMEM((rows, wid), bf16), pltpu.VMEM((wid, rows), bf16), pltpu.SemaphoreType.DMA,
        ],
        compiler_params=pltpu.CompilerParams(vmem_limit_bytes=14 * MIB),
        cost_estimate=pl.CostEstimate(flops=0, bytes_accessed=4 * rows * wid, transcendentals=0),
    )(local_grads)


def split(value):
    high = value.astype(bf16)
    return high, (value - high.astype(f32)).astype(bf16)


def dot(left, right, contract):
    return lax.dot_general(left, right, ((contract[:1], contract[1:]), ((), ())), preferred_element_type=f32)


def dot3(left, right, contract=(1, 0)):
    (lh, ll), (rh, rl) = left, right
    return dot(lh, rh, contract) + (dot(lh, rl, contract) + dot(ll, rh, contract))


def block_order(parts):
    place = {}
    for r in range(parts):
        for c in range(r + 1, parts):
            place[r, c] = len(place)
    for p in range(parts // 2):
        place[p, p] = place[parts - 1 - p, parts - 1 - p] = parts * (parts - 1) // 2 + p
    return place


def triangle_masks():
    row = lax.broadcasted_iota(jnp.int32, (FOLD, FOLD), 0)
    column = lax.broadcasted_iota(jnp.int32, (FOLD, FOLD), 1)
    return row <= column, row == column


def blend_gram_kernel(cut, count, squares, momentum, *refs):
    grads = refs[:STREAMS]
    factor, xh, xl, *parts, packed, extra, high, low, high_t, low_t = refs[STREAMS:]
    columns, hid = xh.shape
    sets = cut.split(parts)
    total_sq = jnp.sum(jnp.sum(squares[...], axis=1, keepdims=True), axis=0, keepdims=True)
    scale = jnp.minimum(1.0, 1.0 / jnp.sqrt(total_sq / count + 1e-06))
    factor[...] = jnp.broadcast_to(scale, factor.shape)
    rows = hid // STREAMS
    if high.shape[0] > columns:
        for target in (high, low):
            target[columns:, :] = jnp.zeros((high.shape[0] - columns, hid), bf16)
        for target in (high_t, low_t):
            target[:, columns:] = jnp.zeros((hid, high.shape[0] - columns), bf16)
    for k in range(STREAMS):
        where = at(k, rows)
        clipped = scale * grads[k][...]
        moved = momentum_decay * momentum[:, where] + clipped
        mixed = clipped + momentum_decay * moved
        for given, target, turned, part in zip((xh, xl), (high, low), (high_t, low_t), split(mixed)):
            given[:, where] = part
            target[:columns, where] = part
            turned[where, :columns] = part.T
    parts, per = hid // FOLD, BLOCK // FOLD
    place = block_order(parts)
    upper, diagonal = triangle_masks()
    extra[...] = jnp.zeros(extra.shape, f32)
    for r in range(hid // BLOCK):
        for c in range(r, hid // BLOCK):
            value = dot3((high_t[at(r, BLOCK), :], low_t[at(r, BLOCK), :]),
                         (high[:, at(c, BLOCK)], low[:, at(c, BLOCK)]))
            for i in range(per):
                for j in range(per):
                    u, v = r * per + i, c * per + j
                    if u > v:
                        continue
                    block, where = value[at(i, FOLD), at(j, FOLD)], at(place[u, v], FOLD)
                    if u == v and u >= parts // 2:
                        line = parts - 1 - u
                        extra[line:line + 1, :] = jnp.sum(jnp.where(diagonal, block, 0.0), axis=0, keepdims=True)
                        block = jnp.where(upper, packed[where, :], block)
                    packed[where, :] = block
    for which, slot, row, whole, rows in cut.pieces(False):
        sets[which][slot][row:row + rows, :] = packed[pl.ds(pl.multiple_of(whole, 8), rows), :]
    for part in sets[0]:
        part[part.shape[0] - EXTRA:, :] = extra[...]


def blend_gram(cut, count, squares, momentum, grads):
    columns, hid = momentum.shape
    shapes = cut.shapes()
    padded = -(-columns // LANES) * LANES
    vmem = pl.BlockSpec(memory_space=pltpu.VMEM)
    return pl.pallas_call(
        functools.partial(blend_gram_kernel, cut, count),
        in_specs=[vmem] * (2 + STREAMS),
        out_specs=[vmem] * (3 + len(shapes)),
        out_shape=[
            jax.ShapeDtypeStruct((8, LANES), f32),
            jax.ShapeDtypeStruct((columns, hid), bf16),
            jax.ShapeDtypeStruct((columns, hid), bf16),
            *shapes,
        ],
        scratch_shapes=[pltpu.VMEM((hid * hid // 2 // LANES, LANES), f32), pltpu.VMEM((EXTRA, LANES), f32)]
        + [pltpu.VMEM((padded, hid), bf16)] * 2
        + [pltpu.VMEM((hid, padded), bf16)] * 2,
        compiler_params=pltpu.CompilerParams(vmem_limit_bytes=30 * MIB),
    )(squares, momentum, *grads)


def chain_kernel(scale, cut, count, given_high, given_low, *refs):
    pieces = refs[:count]
    update, packed, gram, al, ar, pr, tl, xl, yl, x32, y32 = refs[count:]
    columns, hid = update.shape
    sets = cut.split(pieces)
    for which, slot, row, whole, rows in cut.pieces(True):
        packed[pl.ds(pl.multiple_of(whole, 8), rows), :] = sets[which][slot][row:row + rows, :]
    extra = sets[0][0][cut.large:cut.large + EXTRA, :]
    parts = hid // FOLD
    blocks = hid // BLOCK
    pairs = [(r, c) for r in range(blocks) for c in range(r, blocks)]
    per = BLOCK // FOLD
    place = block_order(parts)
    upper, diagonal = triangle_masks()
    row = lax.broadcasted_iota(jnp.int32, (BLOCK, BLOCK), 0)
    eye = (row == lax.broadcasted_iota(jnp.int32, (BLOCK, BLOCK), 1)).astype(f32)

    def piece(r, c):
        value = packed[at(place[min(r, c), max(r, c)], FOLD), :]
        if r > c:
            return value.T
        if r < c:
            return value
        if r < parts // 2:
            return jnp.where(upper, value, value.T)
        line = parts - 1 - r
        return jnp.where(diagonal, extra[line:line + 1, :], jnp.where(upper, value.T, value))

    trace = extra + sum(
        jnp.sum(jnp.where(diagonal, packed[at(place[p, p], FOLD), :], 0.0).reshape(-1, EXTRA, LANES), axis=0)
        for p in range(parts // 2)
    )
    trace = jnp.sum(jnp.sum(trace, axis=1, keepdims=True), axis=0, keepdims=True)
    inverse = 1.0 / (jnp.sqrt(trace) + 1e-07)
    inverse_sq = inverse * inverse

    def store_left(target, rows, c, high, low):
        for k, part in enumerate((high, low, high)):
            target[rows, k * hid + c * BLOCK:k * hid + (c + 1) * BLOCK] = part

    def store_right(target, r, c, high, low):
        for k, part in enumerate((high, high, low)):
            target[k * hid + r * BLOCK:k * hid + (r + 1) * BLOCK, at(c, BLOCK)] = part

    def store(left, right, r, c, value):
        high, low = split(value)
        places = [(r, c, high, low)] + ([(c, r, high.T, low.T)] if r != c else [])
        for i, j, first, second in places:
            if left is not None:
                store_left(left, at(i, BLOCK), j, first, second)
            if right is not None:
                store_right(right, i, j, first, second)

    def symmetric(left, right, r, c):
        return dot(left[at(r, BLOCK), :], right[:, at(c, BLOCK)], (1, 0))

    def apply(left, right, c):
        return dot(left[...], right[:, at(c, BLOCK)], (1, 0))

    for r, c in pairs:
        rows = []
        for i in range(per):
            line = []
            for j in range(per):
                u, v = r * per + i, c * per + j
                line.append(piece(u, v))
            rows.append(jnp.concatenate(line, axis=1))
        value = jnp.concatenate(rows, axis=0) * inverse_sq
        gram[at(r, BLOCK), at(c, BLOCK)] = value
        store(al, ar, r, c, value)
    x, y = xl, yl
    for k, part in enumerate((given_high, given_low, given_high)):
        x[:, at(k, hid)] = part[...]

    for number in range(ITERS - 1):
        for r, c in pairs:
            value = third_coef * symmetric(al, ar, r, c) + second_coef * gram[at(r, BLOCK), at(c, BLOCK)]
            store(None, pr, r, c, value + first_coef * eye if r == c else value)
        for r, c in pairs:
            store(tl, None, r, c, symmetric(al, pr, r, c))
        for c in range(blocks):
            value = apply(x, pr, c)
            if number == ITERS - 2:
                x32[:, at(c, BLOCK)] = value
            store_left(y, slice(None), c, *split(value))
        x, y = y, x
        for r, c in pairs:
            value = symmetric(tl, pr, r, c)
            last = number == ITERS - 2
            store(None if last else al, ar, r, c, value)
            if not last:
                gram[at(r, BLOCK), at(c, BLOCK)] = value
    for c in range(blocks):
        value = apply(x, ar, c)
        y32[:, at(c, BLOCK)] = value
        store_left(y, slice(None), c, *split(value))
    factor = inverse * scale
    for c in range(blocks):
        where = at(c, BLOCK)
        value = first_coef * x32[:, where] + second_coef * y32[:, where] + third_coef * apply(y, ar, c)
        update[:, where] = value * factor


def chain(cut, pieces, high, low, scale):
    columns, hid = high.shape
    vmem = pl.BlockSpec(memory_space=pltpu.VMEM)
    left, right = pltpu.VMEM((hid, 3 * hid), bf16), pltpu.VMEM((3 * hid, hid), bf16)
    slab, full = pltpu.VMEM((columns, 3 * hid), bf16), pltpu.VMEM((columns, hid), f32)
    return pl.pallas_call(
        functools.partial(chain_kernel, scale, cut, len(pieces)),
        in_specs=[vmem] * (2 + len(pieces)),
        out_specs=vmem,
        out_shape=jax.ShapeDtypeStruct((columns, hid), f32),
        scratch_shapes=[
            pltpu.VMEM((hid * hid // 2 // LANES, LANES), f32), pltpu.VMEM((hid, hid), f32),
            left, right, right, left, slab, slab, full, full,
        ],
        compiler_params=pltpu.CompilerParams(vmem_limit_bytes=46 * MIB),
    )(high, low, *pieces)


def body(local_grads, momentum):
    hid, wid = local_grads.shape[2:]
    rows = hid // STREAMS
    ways = [1 if k % 2 == 0 else -1 for k in range(STREAMS)]
    source = pltpu.with_memory_space_constraint(local_grads, pltpu.HBM)
    firsts = first_messages(source, "dp", ways, rows)
    terms = [transposed(source, "dp", way, k * rows, rows) for k, way in enumerate(ways)]
    grads = ring_sum_scatter("dp", ways, firsts, terms)
    squares = sum(jnp.sum((part * part).reshape(-1, 8, rows), axis=0) for part in grads)
    for line in (*two_lines("dp"), Line("expert", lax.axis_size("expert"), 1)):
        squares = line.sum(squares)
    cut = Cut(hid * hid // 2 // LANES, "dp")
    count = hid * wid * lax.axis_size("expert")
    factor, high, low, *parts = blend_gram(cut, count, squares, momentum[0].T, grads)
    new_momentum = momentum_decay * momentum[0].T + factor[0, 0] * jnp.concatenate(grads, axis=1)
    pieces = cut.all_sum(parts)
    update = chain(cut, pieces, high, low, 0.2 * math.sqrt(max(hid, wid)))
    return (new_momentum.T[None], update.T[None])


def solution(mesh):
    return jax.shard_map(
        body,
        mesh=mesh,
        in_specs=(P("expert", "dp", None, None), P("expert", None, "dp")),
        out_specs=(P("expert", None, "dp"), P("expert", None, "dp")),
        check_vma=False,
    )
```

```python
import functools
import math

import jax
import jax.numpy as jnp
from jax import lax
from jax.experimental import pallas as pl
from jax.experimental.pallas import tpu as pltpu
from jax.sharding import PartitionSpec as P

ITERS = 3
STREAMS = 4
FOLD = 128
EXTRA = 8
BLOCK = 256
LANES = 128
MIB = 2**20

first_coef = 3.4445
second_coef = -4.775
third_coef = 2.0315
momentum_decay = 0.95
f32 = jnp.float32
bf16 = jnp.bfloat16


def ring_order(size):
    return list(range(0, size, 2)) + list(range(1, size, 2))[::-1]


def ring_owner(axis, offset):
    size, me = lax.axis_size(axis), lax.axis_index(axis)
    half = lax.div(me, 2)
    position = jnp.where(lax.rem(me, 2) == 0, half, size - 1 - half)
    place = lax.rem(position + offset + size, size)
    return jnp.where(place < (size + 1) // 2, 2 * place, 2 * (size - 1 - place) + 1)


def ring_send(value, axis, way):
    size = lax.axis_size(axis)
    order = ring_order(size)
    return lax.ppermute(value, axis, [(order[p], order[(p + way) % size]) for p in range(size)])


def ring_sum_scatter(axis, ways, firsts, terms):
    held = list(firsts)
    for step in range(lax.axis_size(axis) - 1):
        for k, way in enumerate(ways):
            held[k] = ring_send(held[k], axis, way) + terms[k][step].astype(f32)
    return held


class Line:
    def __init__(self, axis, size, stride):
        self.axis, self.size, self.stride = axis, size, stride

    def digit(self, shift=0):
        own = lax.rem(lax.div(lax.axis_index(self.axis), self.stride), self.size)
        return lax.rem(own + shift + self.size, self.size)

    def send(self, value, shift):
        pairs = []
        for p in range(lax.axis_size(self.axis)):
            digit = p // self.stride % self.size
            pairs.append((p, p + ((digit + shift) % self.size - digit) * self.stride))
        return lax.ppermute(value, self.axis, pairs)

    def everyone(self, value):
        return [value] + [self.send(value, shift) for shift in range(1, self.size)]

    def sum(self, value):
        return sum(self.everyone(value)[1:], value)

    def sum_scatter(self, parts):
        return sum([self.send(parts[shift], shift) for shift in range(1, self.size)], parts[0])


def two_lines(axis):
    size = lax.axis_size(axis)
    inner = 2 if size % 2 == 0 else 1
    return Line(axis, size // inner, inner), Line(axis, inner, 1)


class Cut:
    def __init__(self, rows, axis):
        self.outer, self.inner = two_lines(axis)
        unit = rows // (self.outer.size * self.inner.size)
        self.large = unit - max(8, unit // 24 * 8)
        self.start = self.outer.size * self.inner.size * self.large
        self.quarter = (rows - self.start) // self.outer.size

    def pieces(self, back):
        sign = -1 if back else 1
        outer, inner = self.outer, self.inner
        step = self.large + (EXTRA if back else 0)
        for s in range(outer.size):
            z = outer.digit(sign * s)
            for t in range(inner.size):
                y = inner.digit(sign * t)
                yield 0, t, s * step, (y * outer.size + z) * self.large, self.large
            yield 1, s, 0, self.start + z * self.quarter, self.quarter

    def shapes(self):
        one = jax.ShapeDtypeStruct((self.outer.size * self.large + EXTRA, LANES), f32)
        two = jax.ShapeDtypeStruct((self.quarter, LANES), f32)
        return [one] * self.inner.size + [two] * self.outer.size

    def split(self, refs):
        return refs[:self.inner.size], refs[self.inner.size:]

    def all_sum(self, parts):
        one, two = self.split(parts)
        outer, inner = self.outer, self.inner
        one, two = lax.optimization_barrier((inner.sum_scatter(one), outer.sum_scatter(two)))
        one = [jnp.concatenate([one[at(s, self.large)], one[-EXTRA:]]) for s in range(outer.size)]
        one, two = lax.optimization_barrier((outer.sum_scatter(one), inner.sum(two)))
        one, two = lax.optimization_barrier((outer.everyone(one), two))
        return [*inner.everyone(jnp.concatenate(one, axis=0)), *outer.everyone(two)]


def at(block, size):
    return slice(block * size, (block + 1) * size)


def window(wid, columns):
    spare = LANES - math.gcd(columns, LANES)
    return min(wid, -(-(columns + spare) // LANES) * LANES)


def first_kernel(axis, ways, source, *refs):
    firsts, (held, turned, sems) = refs[:len(ways)], refs[len(ways):]
    columns, rows = firsts[0].shape
    wid, width = source.shape[3], held.shape[2]
    copies, skips = [], []
    for k, way in enumerate(ways):
        begin = ring_owner(axis, -way) * columns
        aligned = pl.multiple_of(jnp.minimum(lax.div(begin, LANES) * LANES, wid - width), LANES)
        skips.append(pl.multiple_of(begin - aligned, math.gcd(columns, LANES)))
        copies.append(pltpu.make_async_copy(
            source.at[0, 0, pl.ds(k * rows, rows), pl.ds(aligned, width)], held.at[k], sems.at[k]
        ))
    for copy in copies:
        copy.start()
    for k, first in enumerate(firsts):
        copies[k].wait()
        turned[...] = held[k].astype(f32).T
        first[...] = turned[pl.ds(skips[k], columns), :]


def first_messages(local_grads, axis, ways, rows):
    wid, size = local_grads.shape[3], lax.axis_size(axis)
    columns = wid // size
    width = window(wid, columns)
    return pl.pallas_call(
        functools.partial(first_kernel, axis, ways),
        in_specs=[pl.BlockSpec(memory_space=pltpu.HBM)],
        out_specs=[pl.BlockSpec(memory_space=pltpu.VMEM)] * len(ways),
        out_shape=[jax.ShapeDtypeStruct((columns, rows), f32)] * len(ways),
        scratch_shapes=[
            pltpu.VMEM((len(ways), rows, width), bf16), pltpu.VMEM((width, rows), f32),
            pltpu.SemaphoreType.DMA((len(ways),)),
        ],
        compiler_params=pltpu.CompilerParams(vmem_limit_bytes=12 * MIB),
        cost_estimate=pl.CostEstimate(flops=0, bytes_accessed=6 * len(ways) * rows * columns, transcendentals=0),
    )(local_grads)


def transpose_kernel(axis, way, start, source, terms, held, turned, sem):
    steps, columns, rows = terms.shape
    copy = pltpu.make_async_copy(source.at[0, 0, pl.ds(start, rows)], held, sem)
    copy.start()
    copy.wait()
    wid = held.shape[1]
    step = 512
    for c in range(0, wid, step):
        width = min(step, wid - c)
        turned[c:c + width, :] = held[:, c:c + width].T
    for step in range(steps):
        owner = ring_owner(axis, -way * (step + 2))
        terms[step] = turned[pl.ds(pl.multiple_of(owner * columns, 16), columns), :]


def transposed(local_grads, axis, way, start, rows):
    wid, size = local_grads.shape[3], lax.axis_size(axis)
    columns = wid // size
    return pl.pallas_call(
        functools.partial(transpose_kernel, axis, way, start),
        in_specs=[pl.BlockSpec(memory_space=pltpu.HBM)],
        out_specs=pl.BlockSpec(memory_space=pltpu.VMEM),
        out_shape=jax.ShapeDtypeStruct((size - 1, columns, rows), local_grads.dtype),
        scratch_shapes=[
            pltpu.VMEM((rows, wid), bf16), pltpu.VMEM((wid, rows), bf16), pltpu.SemaphoreType.DMA,
        ],
        compiler_params=pltpu.CompilerParams(vmem_limit_bytes=14 * MIB),
        cost_estimate=pl.CostEstimate(flops=0, bytes_accessed=4 * rows * wid, transcendentals=0),
    )(local_grads)


def split(value):
    high = value.astype(bf16)
    return high, (value - high.astype(f32)).astype(bf16)


def dot(left, right, contract):
    return lax.dot_general(left, right, ((contract[:1], contract[1:]), ((), ())), preferred_element_type=f32)


def dot3(left, right, contract=(1, 0)):
    (lh, ll), (rh, rl) = left, right
    return dot(lh, rh, contract) + (dot(lh, rl, contract) + dot(ll, rh, contract))


def block_order(parts):
    place = {}
    for r in range(parts):
        for c in range(r + 1, parts):
            place[r, c] = len(place)
    for p in range(parts // 2):
        place[p, p] = place[parts - 1 - p, parts - 1 - p] = parts * (parts - 1) // 2 + p
    return place


def triangle_masks():
    row = lax.broadcasted_iota(jnp.int32, (FOLD, FOLD), 0)
    column = lax.broadcasted_iota(jnp.int32, (FOLD, FOLD), 1)
    return row <= column, row == column


def blend_gram_kernel(cut, count, squares, momentum, *refs):
    grads = refs[:STREAMS]
    factor, xh, xl, *parts, packed, extra, high, low, high_t, low_t = refs[STREAMS:]
    columns, hid = xh.shape
    sets = cut.split(parts)
    total_sq = jnp.sum(jnp.sum(squares[...], axis=1, keepdims=True), axis=0, keepdims=True)
    scale = jnp.minimum(1.0, 1.0 / jnp.sqrt(total_sq / count + 1e-06))
    factor[...] = jnp.broadcast_to(scale, factor.shape)
    rows = hid // STREAMS
    if high.shape[0] > columns:
        for target in (high, low):
            target[columns:, :] = jnp.zeros((high.shape[0] - columns, hid), bf16)
        for target in (high_t, low_t):
            target[:, columns:] = jnp.zeros((hid, high.shape[0] - columns), bf16)
    for k in range(STREAMS):
        where = at(k, rows)
        clipped = scale * grads[k][...]
        moved = momentum_decay * momentum[:, where] + clipped
        mixed = clipped + momentum_decay * moved
        for given, target, turned, part in zip((xh, xl), (high, low), (high_t, low_t), split(mixed)):
            given[:, where] = part
            target[:columns, where] = part
            turned[where, :columns] = part.T
    parts, per = hid // FOLD, BLOCK // FOLD
    place = block_order(parts)
    upper, diagonal = triangle_masks()
    extra[...] = jnp.zeros(extra.shape, f32)
    for r in range(hid // BLOCK):
        for c in range(r, hid // BLOCK):
            value = dot3((high_t[at(r, BLOCK), :], low_t[at(r, BLOCK), :]),
                         (high[:, at(c, BLOCK)], low[:, at(c, BLOCK)]))
            for i in range(per):
                for j in range(per):
                    u, v = r * per + i, c * per + j
                    if u > v:
                        continue
                    block, where = value[at(i, FOLD), at(j, FOLD)], at(place[u, v], FOLD)
                    if u == v and u >= parts // 2:
                        line = parts - 1 - u
                        extra[line:line + 1, :] = jnp.sum(jnp.where(diagonal, block, 0.0), axis=0, keepdims=True)
                        block = jnp.where(upper, packed[where, :], block)
                    packed[where, :] = block
    for which, slot, row, whole, rows in cut.pieces(False):
        sets[which][slot][row:row + rows, :] = packed[pl.ds(pl.multiple_of(whole, 8), rows), :]
    for part in sets[0]:
        part[part.shape[0] - EXTRA:, :] = extra[...]


def blend_gram(cut, count, squares, momentum, grads):
    columns, hid = momentum.shape
    shapes = cut.shapes()
    padded = -(-columns // LANES) * LANES
    vmem = pl.BlockSpec(memory_space=pltpu.VMEM)
    return pl.pallas_call(
        functools.partial(blend_gram_kernel, cut, count),
        in_specs=[vmem] * (2 + STREAMS),
        out_specs=[vmem] * (3 + len(shapes)),
        out_shape=[
            jax.ShapeDtypeStruct((8, LANES), f32),
            jax.ShapeDtypeStruct((columns, hid), bf16),
            jax.ShapeDtypeStruct((columns, hid), bf16),
            *shapes,
        ],
        scratch_shapes=[pltpu.VMEM((hid * hid // 2 // LANES, LANES), f32), pltpu.VMEM((EXTRA, LANES), f32)]
        + [pltpu.VMEM((padded, hid), bf16)] * 2
        + [pltpu.VMEM((hid, padded), bf16)] * 2,
        compiler_params=pltpu.CompilerParams(vmem_limit_bytes=30 * MIB),
    )(squares, momentum, *grads)


def chain_kernel(scale, cut, count, given_high, given_low, *refs):
    pieces = refs[:count]
    update, packed, gram, al, ar, pr, tl, xl, yl, x32, y32 = refs[count:]
    columns, hid = update.shape
    sets = cut.split(pieces)
    for which, slot, row, whole, rows in cut.pieces(True):
        packed[pl.ds(pl.multiple_of(whole, 8), rows), :] = sets[which][slot][row:row + rows, :]
    extra = sets[0][0][cut.large:cut.large + EXTRA, :]
    parts = hid // FOLD
    blocks = hid // BLOCK
    pairs = [(r, c) for r in range(blocks) for c in range(r, blocks)]
    per = BLOCK // FOLD
    place = block_order(parts)
    upper, diagonal = triangle_masks()
    row = lax.broadcasted_iota(jnp.int32, (BLOCK, BLOCK), 0)
    eye = (row == lax.broadcasted_iota(jnp.int32, (BLOCK, BLOCK), 1)).astype(f32)

    def piece(r, c):
        value = packed[at(place[min(r, c), max(r, c)], FOLD), :]
        if r > c:
            return value.T
        if r < c:
            return value
        if r < parts // 2:
            return jnp.where(upper, value, value.T)
        line = parts - 1 - r
        return jnp.where(diagonal, extra[line:line + 1, :], jnp.where(upper, value.T, value))

    trace = extra + sum(
        jnp.sum(jnp.where(diagonal, packed[at(place[p, p], FOLD), :], 0.0).reshape(-1, EXTRA, LANES), axis=0)
        for p in range(parts // 2)
    )
    trace = jnp.sum(jnp.sum(trace, axis=1, keepdims=True), axis=0, keepdims=True)
    inverse = 1.0 / (jnp.sqrt(trace) + 1e-07)
    inverse_sq = inverse * inverse

    def store_left(target, rows, c, high, low):
        for k, part in enumerate((high, low, high)):
            target[rows, k * hid + c * BLOCK:k * hid + (c + 1) * BLOCK] = part

    def store_right(target, r, c, high, low):
        for k, part in enumerate((high, high, low)):
            target[k * hid + r * BLOCK:k * hid + (r + 1) * BLOCK, at(c, BLOCK)] = part

    def store(left, right, r, c, value):
        high, low = split(value)
        places = [(r, c, high, low)] + ([(c, r, high.T, low.T)] if r != c else [])
        for i, j, first, second in places:
            if left is not None:
                store_left(left, at(i, BLOCK), j, first, second)
            if right is not None:
                store_right(right, i, j, first, second)

    def symmetric(left, right, r, c):
        return dot(left[at(r, BLOCK), :], right[:, at(c, BLOCK)], (1, 0))

    def apply(left, right, c):
        return dot(left[...], right[:, at(c, BLOCK)], (1, 0))

    for r, c in pairs:
        rows = []
        for i in range(per):
            line = []
            for j in range(per):
                u, v = r * per + i, c * per + j
                line.append(piece(u, v))
            rows.append(jnp.concatenate(line, axis=1))
        value = jnp.concatenate(rows, axis=0) * inverse_sq
        gram[at(r, BLOCK), at(c, BLOCK)] = value
        store(al, ar, r, c, value)
    x, y = None, yl

    for number in range(ITERS - 1):
        for r, c in pairs:
            value = third_coef * symmetric(al, ar, r, c) + second_coef * gram[at(r, BLOCK), at(c, BLOCK)]
            store(None, pr, r, c, value + first_coef * eye if r == c else value)
        for r, c in pairs:
            store(tl, None, r, c, symmetric(al, pr, r, c))
        for c in range(blocks):
            if x is None:
                value = sum(
                    dot(part[...], pr[at(k, hid), at(c, BLOCK)], (1, 0))
                    for k, part in enumerate((given_high, given_low, given_high))
                )
            else:
                value = apply(x, pr, c)
            if number == ITERS - 2:
                x32[:, at(c, BLOCK)] = value
            store_left(y, slice(None), c, *split(value))
        x, y = y, xl if y is yl else yl
        for r, c in pairs:
            value = symmetric(tl, pr, r, c)
            last = number == ITERS - 2
            store(None if last else al, ar, r, c, value)
            if not last:
                gram[at(r, BLOCK), at(c, BLOCK)] = value
    for c in range(blocks):
        value = apply(x, ar, c)
        y32[:, at(c, BLOCK)] = value
        store_left(y, slice(None), c, *split(value))
    factor = inverse * scale
    for c in range(blocks):
        where = at(c, BLOCK)
        value = first_coef * x32[:, where] + second_coef * y32[:, where] + third_coef * apply(y, ar, c)
        update[:, where] = value * factor


def chain(cut, pieces, high, low, scale):
    columns, hid = high.shape
    vmem = pl.BlockSpec(memory_space=pltpu.VMEM)
    left, right = pltpu.VMEM((hid, 3 * hid), bf16), pltpu.VMEM((3 * hid, hid), bf16)
    slab, full = pltpu.VMEM((columns, 3 * hid), bf16), pltpu.VMEM((columns, hid), f32)
    return pl.pallas_call(
        functools.partial(chain_kernel, scale, cut, len(pieces)),
        in_specs=[vmem] * (2 + len(pieces)),
        out_specs=vmem,
        out_shape=jax.ShapeDtypeStruct((columns, hid), f32),
        scratch_shapes=[
            pltpu.VMEM((hid * hid // 2 // LANES, LANES), f32), pltpu.VMEM((hid, hid), f32),
            left, right, right, left, slab, slab, full, full,
        ],
        compiler_params=pltpu.CompilerParams(vmem_limit_bytes=46 * MIB),
    )(high, low, *pieces)


def body(local_grads, momentum):
    hid, wid = local_grads.shape[2:]
    rows = hid // STREAMS
    ways = [1 if k % 2 == 0 else -1 for k in range(STREAMS)]
    source = pltpu.with_memory_space_constraint(local_grads, pltpu.HBM)
    firsts = first_messages(source, "dp", ways, rows)
    terms = [transposed(source, "dp", way, k * rows, rows) for k, way in enumerate(ways)]
    grads = ring_sum_scatter("dp", ways, firsts, terms)
    squares = sum(jnp.sum((part * part).reshape(-1, 8, rows), axis=0) for part in grads)
    for line in (*two_lines("dp"), Line("expert", lax.axis_size("expert"), 1)):
        squares = line.sum(squares)
    cut = Cut(hid * hid // 2 // LANES, "dp")
    count = hid * wid * lax.axis_size("expert")
    factor, high, low, *parts = blend_gram(cut, count, squares, momentum[0].T, grads)
    new_momentum = momentum_decay * momentum[0].T + factor[0, 0] * jnp.concatenate(grads, axis=1)
    pieces = cut.all_sum(parts)
    update = chain(cut, pieces, high, low, 0.2 * math.sqrt(max(hid, wid)))
    return (new_momentum.T[None], update.T[None])


def solution(mesh):
    return jax.shard_map(
        body,
        mesh=mesh,
        in_specs=(P("expert", "dp", None, None), P("expert", None, "dp")),
        out_specs=(P("expert", None, "dp"), P("expert", None, "dp")),
        check_vma=False,
    )
```

```python
import functools
import math

import jax
import jax.numpy as jnp
from jax import lax
from jax.experimental import pallas as pl
from jax.experimental.pallas import tpu as pltpu
from jax.sharding import PartitionSpec as P

ITERS = 3
STREAMS = 4
FOLD = 128
EXTRA = 8
BLOCK = 256
LANES = 128
MIB = 2**20

first_coef = 3.4445
second_coef = -4.775
third_coef = 2.0315
momentum_decay = 0.95
f32 = jnp.float32
bf16 = jnp.bfloat16


def ring_order(size):
    return list(range(0, size, 2)) + list(range(1, size, 2))[::-1]


def ring_owner(axis, offset):
    size, me = lax.axis_size(axis), lax.axis_index(axis)
    half = lax.div(me, 2)
    position = jnp.where(lax.rem(me, 2) == 0, half, size - 1 - half)
    place = lax.rem(position + offset + size, size)
    return jnp.where(place < (size + 1) // 2, 2 * place, 2 * (size - 1 - place) + 1)


def ring_send(value, axis, way):
    size = lax.axis_size(axis)
    order = ring_order(size)
    return lax.ppermute(value, axis, [(order[p], order[(p + way) % size]) for p in range(size)])


def ring_sum_scatter(axis, ways, firsts, terms):
    held = list(firsts)
    for step in range(lax.axis_size(axis) - 1):
        for k, way in enumerate(ways):
            held[k] = ring_send(held[k], axis, way) + terms[k][step].astype(f32)
    return held


class Line:
    def __init__(self, axis, size, stride):
        self.axis, self.size, self.stride = axis, size, stride

    def digit(self, shift=0):
        own = lax.rem(lax.div(lax.axis_index(self.axis), self.stride), self.size)
        return lax.rem(own + shift + self.size, self.size)

    def send(self, value, shift):
        pairs = []
        for p in range(lax.axis_size(self.axis)):
            digit = p // self.stride % self.size
            pairs.append((p, p + ((digit + shift) % self.size - digit) * self.stride))
        return lax.ppermute(value, self.axis, pairs)

    def everyone(self, value):
        return [value] + [self.send(value, shift) for shift in range(1, self.size)]

    def sum(self, value):
        return sum(self.everyone(value)[1:], value)

    def sum_scatter(self, parts):
        return sum([self.send(parts[shift], shift) for shift in range(1, self.size)], parts[0])


def two_lines(axis):
    size = lax.axis_size(axis)
    inner = 2 if size % 2 == 0 else 1
    return Line(axis, size // inner, inner), Line(axis, inner, 1)


class Cut:
    def __init__(self, rows, axis):
        self.outer, self.inner = two_lines(axis)
        unit = rows // (self.outer.size * self.inner.size)
        self.large = unit - max(8, unit // 24 * 8)
        self.start = self.outer.size * self.inner.size * self.large
        self.quarter = (rows - self.start) // self.outer.size

    def pieces(self, back):
        sign = -1 if back else 1
        outer, inner = self.outer, self.inner
        step = self.large + (EXTRA if back else 0)
        for s in range(outer.size):
            z = outer.digit(sign * s)
            for t in range(inner.size):
                y = inner.digit(sign * t)
                yield 0, t, s * step, (y * outer.size + z) * self.large, self.large
            yield 1, s, 0, self.start + z * self.quarter, self.quarter

    def shapes(self):
        one = jax.ShapeDtypeStruct((self.outer.size * self.large + EXTRA, LANES), f32)
        two = jax.ShapeDtypeStruct((self.quarter, LANES), f32)
        return [one] * self.inner.size + [two] * self.outer.size

    def split(self, refs):
        return refs[:self.inner.size], refs[self.inner.size:]

    def all_sum(self, parts):
        one, two = self.split(parts)
        outer, inner = self.outer, self.inner
        one, two = lax.optimization_barrier((inner.sum_scatter(one), outer.sum_scatter(two)))
        one = [jnp.concatenate([one[at(s, self.large)], one[-EXTRA:]]) for s in range(outer.size)]
        one, two = lax.optimization_barrier((outer.sum_scatter(one), inner.sum(two)))
        one, two = lax.optimization_barrier((outer.everyone(one), two))
        return [*inner.everyone(jnp.concatenate(one, axis=0)), *outer.everyone(two)]


def at(block, size):
    return slice(block * size, (block + 1) * size)


def window(wid, columns):
    spare = LANES - math.gcd(columns, LANES)
    return min(wid, -(-(columns + spare) // LANES) * LANES)


def first_kernel(axis, ways, source, *refs):
    firsts, (held, turned, sems) = refs[:len(ways)], refs[len(ways):]
    columns, rows = firsts[0].shape
    wid, width = source.shape[3], held.shape[2]
    copies, skips = [], []
    for k, way in enumerate(ways):
        begin = ring_owner(axis, -way) * columns
        aligned = pl.multiple_of(jnp.minimum(lax.div(begin, LANES) * LANES, wid - width), LANES)
        skips.append(pl.multiple_of(begin - aligned, math.gcd(columns, LANES)))
        copies.append(pltpu.make_async_copy(
            source.at[0, 0, pl.ds(k * rows, rows), pl.ds(aligned, width)], held.at[k], sems.at[k]
        ))
    for copy in copies:
        copy.start()
    for k, first in enumerate(firsts):
        copies[k].wait()
        turned[...] = held[k].astype(f32).T
        first[...] = turned[pl.ds(skips[k], columns), :]


def first_messages(local_grads, axis, ways, rows):
    wid, size = local_grads.shape[3], lax.axis_size(axis)
    columns = wid // size
    width = window(wid, columns)
    return pl.pallas_call(
        functools.partial(first_kernel, axis, ways),
        in_specs=[pl.BlockSpec(memory_space=pltpu.HBM)],
        out_specs=[pl.BlockSpec(memory_space=pltpu.VMEM)] * len(ways),
        out_shape=[jax.ShapeDtypeStruct((columns, rows), f32)] * len(ways),
        scratch_shapes=[
            pltpu.VMEM((len(ways), rows, width), bf16), pltpu.VMEM((width, rows), f32),
            pltpu.SemaphoreType.DMA((len(ways),)),
        ],
        compiler_params=pltpu.CompilerParams(vmem_limit_bytes=12 * MIB),
        cost_estimate=pl.CostEstimate(flops=0, bytes_accessed=6 * len(ways) * rows * columns, transcendentals=0),
    )(local_grads)


def transpose_kernel(axis, way, start, source, terms, held, turned, sem):
    steps, columns, rows = terms.shape
    copy = pltpu.make_async_copy(source.at[0, 0, pl.ds(start, rows)], held, sem)
    copy.start()
    copy.wait()
    wid = held.shape[1]
    step = 512
    for c in range(0, wid, step):
        width = min(step, wid - c)
        turned[c:c + width, :] = held[:, c:c + width].T
    for step in range(steps):
        owner = ring_owner(axis, -way * (step + 2))
        terms[step] = turned[pl.ds(pl.multiple_of(owner * columns, 16), columns), :]


def transposed(local_grads, axis, way, start, rows):
    wid, size = local_grads.shape[3], lax.axis_size(axis)
    columns = wid // size
    return pl.pallas_call(
        functools.partial(transpose_kernel, axis, way, start),
        in_specs=[pl.BlockSpec(memory_space=pltpu.HBM)],
        out_specs=pl.BlockSpec(memory_space=pltpu.VMEM),
        out_shape=jax.ShapeDtypeStruct((size - 1, columns, rows), local_grads.dtype),
        scratch_shapes=[
            pltpu.VMEM((rows, wid), bf16), pltpu.VMEM((wid, rows), bf16), pltpu.SemaphoreType.DMA,
        ],
        compiler_params=pltpu.CompilerParams(vmem_limit_bytes=14 * MIB),
        cost_estimate=pl.CostEstimate(flops=0, bytes_accessed=4 * rows * wid, transcendentals=0),
    )(local_grads)


def split(value):
    high = value.astype(bf16)
    return high, (value - high.astype(f32)).astype(bf16)


def dot(left, right, contract):
    return lax.dot_general(left, right, ((contract[:1], contract[1:]), ((), ())), preferred_element_type=f32)


def dot3(left, right, contract=(1, 0)):
    (lh, ll), (rh, rl) = left, right
    return dot(lh, rh, contract) + (dot(lh, rl, contract) + dot(ll, rh, contract))


def block_order(parts):
    place = {}
    for r in range(parts):
        for c in range(r + 1, parts):
            place[r, c] = len(place)
    for p in range(parts // 2):
        place[p, p] = place[parts - 1 - p, parts - 1 - p] = parts * (parts - 1) // 2 + p
    return place


def triangle_masks():
    row = lax.broadcasted_iota(jnp.int32, (FOLD, FOLD), 0)
    column = lax.broadcasted_iota(jnp.int32, (FOLD, FOLD), 1)
    return row <= column, row == column


def blend_gram_kernel(cut, count, squares, momentum, *refs):
    grads = refs[:STREAMS]
    factor, xh, xl, *parts, packed, extra, high, low, high_t, low_t = refs[STREAMS:]
    columns, hid = xh.shape
    sets = cut.split(parts)
    total_sq = jnp.sum(jnp.sum(squares[...], axis=1, keepdims=True), axis=0, keepdims=True)
    scale = jnp.minimum(1.0, 1.0 / jnp.sqrt(total_sq / count + 1e-06))
    factor[...] = jnp.broadcast_to(scale, factor.shape)
    rows = hid // STREAMS
    if high.shape[0] > columns:
        for target in (high, low):
            target[columns:, :] = jnp.zeros((high.shape[0] - columns, hid), bf16)
        for target in (high_t, low_t):
            target[:, columns:] = jnp.zeros((hid, high.shape[0] - columns), bf16)
    for k in range(STREAMS):
        where = at(k, rows)
        clipped = scale * grads[k][...]
        moved = momentum_decay * momentum[:, where] + clipped
        mixed = clipped + momentum_decay * moved
        for given, target, turned, part in zip((xh, xl), (high, low), (high_t, low_t), split(mixed)):
            given[:, where] = part
            target[:columns, where] = part
            turned[where, :columns] = part.T
    parts, per = hid // FOLD, BLOCK // FOLD
    place = block_order(parts)
    upper, diagonal = triangle_masks()
    extra[...] = jnp.zeros(extra.shape, f32)
    for r in range(hid // BLOCK):
        for c in range(r, hid // BLOCK):
            value = dot3((high_t[at(r, BLOCK), :], low_t[at(r, BLOCK), :]),
                         (high[:, at(c, BLOCK)], low[:, at(c, BLOCK)]))
            for i in range(per):
                for j in range(per):
                    u, v = r * per + i, c * per + j
                    if u > v:
                        continue
                    block, where = value[at(i, FOLD), at(j, FOLD)], at(place[u, v], FOLD)
                    if u == v and u >= parts // 2:
                        line = parts - 1 - u
                        extra[line:line + 1, :] = jnp.sum(jnp.where(diagonal, block, 0.0), axis=0, keepdims=True)
                        block = jnp.where(upper, packed[where, :], block)
                    packed[where, :] = block
    for which, slot, row, whole, rows in cut.pieces(False):
        sets[which][slot][row:row + rows, :] = packed[pl.ds(pl.multiple_of(whole, 8), rows), :]
    for part in sets[0]:
        part[part.shape[0] - EXTRA:, :] = extra[...]


def blend_gram(cut, count, squares, momentum, grads):
    columns, hid = momentum.shape
    shapes = cut.shapes()
    padded = -(-columns // LANES) * LANES
    vmem = pl.BlockSpec(memory_space=pltpu.VMEM)
    return pl.pallas_call(
        functools.partial(blend_gram_kernel, cut, count),
        in_specs=[vmem] * (2 + STREAMS),
        out_specs=[vmem] * (3 + len(shapes)),
        out_shape=[
            jax.ShapeDtypeStruct((1, hid), f32),
            jax.ShapeDtypeStruct((columns, hid), bf16),
            jax.ShapeDtypeStruct((columns, hid), bf16),
            *shapes,
        ],
        scratch_shapes=[pltpu.VMEM((hid * hid // 2 // LANES, LANES), f32), pltpu.VMEM((EXTRA, LANES), f32)]
        + [pltpu.VMEM((padded, hid), bf16)] * 2
        + [pltpu.VMEM((hid, padded), bf16)] * 2,
        compiler_params=pltpu.CompilerParams(vmem_limit_bytes=30 * MIB),
    )(squares, momentum, *grads)


def chain_kernel(scale, cut, count, given_high, given_low, *refs):
    pieces = refs[:count]
    update, packed, gram, al, ar, pr, tl, xl, yl, x32, y32 = refs[count:]
    columns, hid = update.shape
    sets = cut.split(pieces)
    for which, slot, row, whole, rows in cut.pieces(True):
        packed[pl.ds(pl.multiple_of(whole, 8), rows), :] = sets[which][slot][row:row + rows, :]
    extra = sets[0][0][cut.large:cut.large + EXTRA, :]
    parts = hid // FOLD
    blocks = hid // BLOCK
    pairs = [(r, c) for r in range(blocks) for c in range(r, blocks)]
    per = BLOCK // FOLD
    place = block_order(parts)
    upper, diagonal = triangle_masks()
    row = lax.broadcasted_iota(jnp.int32, (BLOCK, BLOCK), 0)
    eye = (row == lax.broadcasted_iota(jnp.int32, (BLOCK, BLOCK), 1)).astype(f32)

    def piece(r, c):
        value = packed[at(place[min(r, c), max(r, c)], FOLD), :]
        if r > c:
            return value.T
        if r < c:
            return value
        if r < parts // 2:
            return jnp.where(upper, value, value.T)
        line = parts - 1 - r
        return jnp.where(diagonal, extra[line:line + 1, :], jnp.where(upper, value.T, value))

    trace = extra + sum(
        jnp.sum(jnp.where(diagonal, packed[at(place[p, p], FOLD), :], 0.0).reshape(-1, EXTRA, LANES), axis=0)
        for p in range(parts // 2)
    )
    trace = jnp.sum(jnp.sum(trace, axis=1, keepdims=True), axis=0, keepdims=True)
    inverse = 1.0 / (jnp.sqrt(trace) + 1e-07)
    inverse_sq = inverse * inverse

    def store_left(target, rows, c, high, low):
        for k, part in enumerate((high, low, high)):
            target[rows, k * hid + c * BLOCK:k * hid + (c + 1) * BLOCK] = part

    def store_right(target, r, c, high, low):
        for k, part in enumerate((high, high, low)):
            target[k * hid + r * BLOCK:k * hid + (r + 1) * BLOCK, at(c, BLOCK)] = part

    def store(left, right, r, c, value):
        high, low = split(value)
        places = [(r, c, high, low)] + ([(c, r, high.T, low.T)] if r != c else [])
        for i, j, first, second in places:
            if left is not None:
                store_left(left, at(i, BLOCK), j, first, second)
            if right is not None:
                store_right(right, i, j, first, second)

    def symmetric(left, right, r, c):
        return dot(left[at(r, BLOCK), :], right[:, at(c, BLOCK)], (1, 0))

    tall = columns // -(-columns // BLOCK)
    spans = [slice(begin, min(begin + tall, columns)) for begin in range(0, columns, tall)]

    def apply(left, right, c):
        for rows in spans:
            if left is None:
                yield rows, sum(
                    dot(part[rows, :], right[at(k, hid), at(c, BLOCK)], (1, 0))
                    for k, part in enumerate((given_high, given_low, given_high))
                )
            else:
                yield rows, dot(left[rows, :], right[:, at(c, BLOCK)], (1, 0))

    for r, c in pairs:
        rows = []
        for i in range(per):
            line = []
            for j in range(per):
                u, v = r * per + i, c * per + j
                line.append(piece(u, v))
            rows.append(jnp.concatenate(line, axis=1))
        value = jnp.concatenate(rows, axis=0) * inverse_sq
        gram[at(r, BLOCK), at(c, BLOCK)] = value
        store(al, ar, r, c, value)
    x, y = None, yl

    for number in range(ITERS - 1):
        for r, c in pairs:
            value = third_coef * symmetric(al, ar, r, c) + second_coef * gram[at(r, BLOCK), at(c, BLOCK)]
            store(None, pr, r, c, value + first_coef * eye if r == c else value)
        for r, c in pairs:
            store(tl, None, r, c, symmetric(al, pr, r, c))
        for c in range(blocks):
            for rows, value in apply(x, pr, c):
                if number == ITERS - 2:
                    x32[rows, at(c, BLOCK)] = value
                store_left(y, rows, c, *split(value))
        x, y = y, xl if y is yl else yl
        for r, c in pairs:
            value = symmetric(tl, pr, r, c)
            last = number == ITERS - 2
            store(None if last else al, ar, r, c, value)
            if not last:
                gram[at(r, BLOCK), at(c, BLOCK)] = value
    for c in range(blocks):
        for rows, value in apply(x, ar, c):
            y32[rows, at(c, BLOCK)] = value
            store_left(y, rows, c, *split(value))
    factor = inverse * scale
    for c in range(blocks):
        where = at(c, BLOCK)
        for rows, value in apply(y, ar, c):
            value = first_coef * x32[rows, where] + second_coef * y32[rows, where] + third_coef * value
            update[rows, where] = value * factor


def chain(cut, pieces, high, low, scale):
    columns, hid = high.shape
    vmem = pl.BlockSpec(memory_space=pltpu.VMEM)
    left, right = pltpu.VMEM((hid, 3 * hid), bf16), pltpu.VMEM((3 * hid, hid), bf16)
    slab, full = pltpu.VMEM((columns, 3 * hid), bf16), pltpu.VMEM((columns, hid), f32)
    return pl.pallas_call(
        functools.partial(chain_kernel, scale, cut, len(pieces)),
        in_specs=[vmem] * (2 + len(pieces)),
        out_specs=vmem,
        out_shape=jax.ShapeDtypeStruct((columns, hid), f32),
        scratch_shapes=[
            pltpu.VMEM((hid * hid // 2 // LANES, LANES), f32), pltpu.VMEM((hid, hid), f32),
            left, right, right, left, slab, slab, full, full,
        ],
        compiler_params=pltpu.CompilerParams(vmem_limit_bytes=46 * MIB),
    )(high, low, *pieces)


def body(local_grads, momentum):
    hid, wid = local_grads.shape[2:]
    rows = hid // STREAMS
    ways = [1 if k % 2 == 0 else -1 for k in range(STREAMS)]
    source = pltpu.with_memory_space_constraint(local_grads, pltpu.HBM)
    firsts = first_messages(source, "dp", ways, rows)
    terms = [transposed(source, "dp", way, k * rows, rows) for k, way in enumerate(ways)]
    grads = ring_sum_scatter("dp", ways, firsts, terms)
    squares = sum(jnp.sum((part * part).reshape(-1, 8, rows), axis=0) for part in grads)
    for line in (*two_lines("dp"), Line("expert", lax.axis_size("expert"), 1)):
        squares = line.sum(squares)
    cut = Cut(hid * hid // 2 // LANES, "dp")
    count = hid * wid * lax.axis_size("expert")
    factor, high, low, *parts = blend_gram(cut, count, squares, momentum[0].T, grads)
    new_momentum = momentum_decay * momentum[0].T + factor * jnp.concatenate(grads, axis=1)
    pieces = cut.all_sum(parts)
    update = chain(cut, pieces, high, low, 0.2 * math.sqrt(max(hid, wid)))
    return (new_momentum.T[None], update.T[None])


def solution(mesh):
    return jax.shard_map(
        body,
        mesh=mesh,
        in_specs=(P("expert", "dp", None, None), P("expert", None, "dp")),
        out_specs=(P("expert", None, "dp"), P("expert", None, "dp")),
        check_vma=False,
    )
```

```python
import functools
import math

import jax
import jax.numpy as jnp
from jax import lax
from jax.experimental import pallas as pl
from jax.experimental.pallas import tpu as pltpu
from jax.sharding import PartitionSpec as P

ITERS = 3
STREAMS = 4
FOLD = 128
EXTRA = 8
BLOCK = 256
LANES = 128
MIB = 2**20

first_coef = 3.4445
second_coef = -4.775
third_coef = 2.0315
momentum_decay = 0.95
f32 = jnp.float32
bf16 = jnp.bfloat16


def ring_order(size):
    return list(range(0, size, 2)) + list(range(1, size, 2))[::-1]


def ring_owner(axis, offset):
    size, me = lax.axis_size(axis), lax.axis_index(axis)
    half = lax.div(me, 2)
    position = jnp.where(lax.rem(me, 2) == 0, half, size - 1 - half)
    place = lax.rem(position + offset + size, size)
    return jnp.where(place < (size + 1) // 2, 2 * place, 2 * (size - 1 - place) + 1)


def ring_send(value, axis, way):
    size = lax.axis_size(axis)
    order = ring_order(size)
    return lax.ppermute(value, axis, [(order[p], order[(p + way) % size]) for p in range(size)])


def ring_sum_scatter(axis, ways, firsts, terms):
    held = list(firsts)
    for step in range(lax.axis_size(axis) - 1):
        for k, way in enumerate(ways):
            held[k] = ring_send(held[k], axis, way) + terms[k][step].astype(f32)
    return held


class Line:
    def __init__(self, axis, size, stride):
        self.axis, self.size, self.stride = axis, size, stride

    def digit(self, shift=0):
        own = lax.rem(lax.div(lax.axis_index(self.axis), self.stride), self.size)
        return lax.rem(own + shift + self.size, self.size)

    def send(self, value, shift):
        pairs = []
        for p in range(lax.axis_size(self.axis)):
            digit = p // self.stride % self.size
            pairs.append((p, p + ((digit + shift) % self.size - digit) * self.stride))
        return lax.ppermute(value, self.axis, pairs)

    def everyone(self, value):
        return [value] + [self.send(value, shift) for shift in range(1, self.size)]

    def sum(self, value):
        return sum(self.everyone(value)[1:], value)

    def sum_scatter(self, parts):
        return sum([self.send(parts[shift], shift) for shift in range(1, self.size)], parts[0])


def two_lines(axis):
    size = lax.axis_size(axis)
    inner = 2 if size % 2 == 0 else 1
    return Line(axis, size // inner, inner), Line(axis, inner, 1)


class Cut:
    def __init__(self, rows, axis):
        self.outer, self.inner = two_lines(axis)
        unit = rows // (self.outer.size * self.inner.size)
        self.large = unit - max(8, unit // 24 * 8)
        self.start = self.outer.size * self.inner.size * self.large
        self.quarter = (rows - self.start) // self.outer.size

    def pieces(self, back):
        sign = -1 if back else 1
        outer, inner = self.outer, self.inner
        step = self.large + (EXTRA if back else 0)
        for s in range(outer.size):
            z = outer.digit(sign * s)
            for t in range(inner.size):
                y = inner.digit(sign * t)
                yield 0, t, s * step, (y * outer.size + z) * self.large, self.large
            yield 1, s, 0, self.start + z * self.quarter, self.quarter

    def shapes(self):
        one = jax.ShapeDtypeStruct((self.outer.size * self.large + EXTRA, LANES), f32)
        two = jax.ShapeDtypeStruct((self.quarter, LANES), f32)
        return [one] * self.inner.size + [two] * self.outer.size

    def split(self, refs):
        return refs[:self.inner.size], refs[self.inner.size:]

    def all_sum(self, parts):
        one, two = self.split(parts)
        outer, inner = self.outer, self.inner
        one, two = lax.optimization_barrier((inner.sum_scatter(one), outer.sum_scatter(two)))
        one = [jnp.concatenate([one[at(s, self.large)], one[-EXTRA:]]) for s in range(outer.size)]
        one, two = lax.optimization_barrier((outer.sum_scatter(one), inner.sum(two)))
        one, two = lax.optimization_barrier((outer.everyone(one), two))
        return [*inner.everyone(jnp.concatenate(one, axis=0)), *outer.everyone(two)]


def at(block, size):
    return slice(block * size, (block + 1) * size)


def window(wid, columns):
    spare = LANES - math.gcd(columns, LANES)
    return min(wid, -(-(columns + spare) // LANES) * LANES)


def first_kernel(axis, ways, source, *refs):
    firsts, (held, turned, sems) = refs[:len(ways)], refs[len(ways):]
    columns, rows = firsts[0].shape
    wid, width = source.shape[3], held.shape[2]
    copies, skips = [], []
    for k, way in enumerate(ways):
        begin = ring_owner(axis, -way) * columns
        aligned = pl.multiple_of(jnp.minimum(lax.div(begin, LANES) * LANES, wid - width), LANES)
        skips.append(pl.multiple_of(begin - aligned, math.gcd(columns, LANES)))
        copies.append(pltpu.make_async_copy(
            source.at[0, 0, pl.ds(k * rows, rows), pl.ds(aligned, width)], held.at[k], sems.at[k]
        ))
    for copy in copies:
        copy.start()
    for k, first in enumerate(firsts):
        copies[k].wait()
        turned[...] = held[k].astype(f32).T
        first[...] = turned[pl.ds(skips[k], columns), :]


def first_messages(local_grads, axis, ways, rows):
    wid, size = local_grads.shape[3], lax.axis_size(axis)
    columns = wid // size
    width = window(wid, columns)
    return pl.pallas_call(
        functools.partial(first_kernel, axis, ways),
        in_specs=[pl.BlockSpec(memory_space=pltpu.HBM)],
        out_specs=[pl.BlockSpec(memory_space=pltpu.VMEM)] * len(ways),
        out_shape=[jax.ShapeDtypeStruct((columns, rows), f32)] * len(ways),
        scratch_shapes=[
            pltpu.VMEM((len(ways), rows, width), bf16), pltpu.VMEM((width, rows), f32),
            pltpu.SemaphoreType.DMA((len(ways),)),
        ],
        compiler_params=pltpu.CompilerParams(vmem_limit_bytes=12 * MIB),
        cost_estimate=pl.CostEstimate(flops=0, bytes_accessed=6 * len(ways) * rows * columns, transcendentals=0),
    )(local_grads)


def transpose_kernel(axis, way, start, source, terms, held, turned, sem):
    steps, columns, rows = terms.shape
    copy = pltpu.make_async_copy(source.at[0, 0, pl.ds(start, rows)], held, sem)
    copy.start()
    copy.wait()
    wid = held.shape[1]
    step = 512
    for c in range(0, wid, step):
        width = min(step, wid - c)
        turned[c:c + width, :] = held[:, c:c + width].T
    for step in range(steps):
        owner = ring_owner(axis, -way * (step + 2))
        terms[step] = turned[pl.ds(pl.multiple_of(owner * columns, 16), columns), :]


def transposed(local_grads, axis, way, start, rows):
    wid, size = local_grads.shape[3], lax.axis_size(axis)
    columns = wid // size
    return pl.pallas_call(
        functools.partial(transpose_kernel, axis, way, start),
        in_specs=[pl.BlockSpec(memory_space=pltpu.HBM)],
        out_specs=pl.BlockSpec(memory_space=pltpu.VMEM),
        out_shape=jax.ShapeDtypeStruct((size - 1, columns, rows), local_grads.dtype),
        scratch_shapes=[
            pltpu.VMEM((rows, wid), bf16), pltpu.VMEM((wid, rows), bf16), pltpu.SemaphoreType.DMA,
        ],
        compiler_params=pltpu.CompilerParams(vmem_limit_bytes=14 * MIB),
        cost_estimate=pl.CostEstimate(flops=0, bytes_accessed=4 * rows * wid, transcendentals=0),
    )(local_grads)


def split(value):
    high = value.astype(bf16)
    return high, (value - high.astype(f32)).astype(bf16)


def dot(left, right, contract):
    return lax.dot_general(left, right, ((contract[:1], contract[1:]), ((), ())), preferred_element_type=f32)


def dot3(left, right, contract=(1, 0)):
    (lh, ll), (rh, rl) = left, right
    return dot(lh, rh, contract) + (dot(lh, rl, contract) + dot(ll, rh, contract))


def block_order(parts):
    place = {}
    for r in range(parts):
        for c in range(r + 1, parts):
            place[r, c] = len(place)
    for p in range(parts // 2):
        place[p, p] = place[parts - 1 - p, parts - 1 - p] = parts * (parts - 1) // 2 + p
    return place


def triangle_masks():
    row = lax.broadcasted_iota(jnp.int32, (FOLD, FOLD), 0)
    column = lax.broadcasted_iota(jnp.int32, (FOLD, FOLD), 1)
    return row <= column, row == column


def blend_gram_kernel(cut, count, squares, momentum, *refs):
    grads = refs[:STREAMS]
    factor, xh, xl, *parts, packed, extra, high, low, high_t, low_t = refs[STREAMS:]
    columns, hid = xh.shape
    sets = cut.split(parts)
    total_sq = jnp.sum(jnp.sum(squares[...], axis=1, keepdims=True), axis=0, keepdims=True)
    scale = jnp.minimum(1.0, 1.0 / jnp.sqrt(total_sq / count + 1e-06))
    factor[...] = jnp.broadcast_to(scale, factor.shape)
    rows = hid // STREAMS
    if high.shape[0] > columns:
        for target in (high, low):
            target[columns:, :] = jnp.zeros((high.shape[0] - columns, hid), bf16)
        for target in (high_t, low_t):
            target[:, columns:] = jnp.zeros((hid, high.shape[0] - columns), bf16)
    for k in range(STREAMS):
        where = at(k, rows)
        clipped = scale * grads[k][...]
        moved = momentum_decay * momentum[:, where] + clipped
        mixed = clipped + momentum_decay * moved
        for given, target, turned, part in zip((xh, xl), (high, low), (high_t, low_t), split(mixed)):
            given[:, where] = part
            target[:columns, where] = part
            turned[where, :columns] = part.T
    parts, per = hid // FOLD, BLOCK // FOLD
    place = block_order(parts)
    upper, diagonal = triangle_masks()
    extra[...] = jnp.zeros(extra.shape, f32)
    for r in range(hid // BLOCK):
        for c in range(r, hid // BLOCK):
            value = dot3((high_t[at(r, BLOCK), :], low_t[at(r, BLOCK), :]),
                         (high[:, at(c, BLOCK)], low[:, at(c, BLOCK)]))
            for i in range(per):
                for j in range(per):
                    u, v = r * per + i, c * per + j
                    if u > v:
                        continue
                    block, where = value[at(i, FOLD), at(j, FOLD)], at(place[u, v], FOLD)
                    if u == v and u >= parts // 2:
                        line = parts - 1 - u
                        extra[line:line + 1, :] = jnp.sum(jnp.where(diagonal, block, 0.0), axis=0, keepdims=True)
                        block = jnp.where(upper, packed[where, :], block)
                    packed[where, :] = block
    for which, slot, row, whole, rows in cut.pieces(False):
        sets[which][slot][row:row + rows, :] = packed[pl.ds(pl.multiple_of(whole, 8), rows), :]
    for part in sets[0]:
        part[part.shape[0] - EXTRA:, :] = extra[...]


def blend_gram(cut, count, squares, momentum, grads):
    columns, hid = momentum.shape
    shapes = cut.shapes()
    padded = -(-columns // LANES) * LANES
    vmem = pl.BlockSpec(memory_space=pltpu.VMEM)
    return pl.pallas_call(
        functools.partial(blend_gram_kernel, cut, count),
        in_specs=[vmem] * (2 + STREAMS),
        out_specs=[vmem] * (3 + len(shapes)),
        out_shape=[
            jax.ShapeDtypeStruct((1, hid), f32),
            jax.ShapeDtypeStruct((columns, hid), bf16),
            jax.ShapeDtypeStruct((columns, hid), bf16),
            *shapes,
        ],
        scratch_shapes=[pltpu.VMEM((hid * hid // 2 // LANES, LANES), f32), pltpu.VMEM((EXTRA, LANES), f32)]
        + [pltpu.VMEM((padded, hid), bf16)] * 2
        + [pltpu.VMEM((hid, padded), bf16)] * 2,
        compiler_params=pltpu.CompilerParams(vmem_limit_bytes=30 * MIB),
    )(squares, momentum, *grads)


def chain_kernel(scale, cut, count, given_high, given_low, *refs):
    pieces = refs[:count]
    update, packed, gram, al, ar, pr, tl, xl, yl, x32, y32 = refs[count:]
    columns, hid = update.shape
    sets = cut.split(pieces)
    for which, slot, row, whole, rows in cut.pieces(True):
        packed[pl.ds(pl.multiple_of(whole, 8), rows), :] = sets[which][slot][row:row + rows, :]
    extra = sets[0][0][cut.large:cut.large + EXTRA, :]
    parts = hid // FOLD
    blocks = hid // BLOCK
    pairs = [(r, c) for r in range(blocks) for c in range(r, blocks)]
    per = BLOCK // FOLD
    place = block_order(parts)
    upper, diagonal = triangle_masks()
    row = lax.broadcasted_iota(jnp.int32, (BLOCK, BLOCK), 0)
    eye = (row == lax.broadcasted_iota(jnp.int32, (BLOCK, BLOCK), 1)).astype(f32)

    def piece(r, c):
        value = packed[at(place[min(r, c), max(r, c)], FOLD), :]
        if r > c:
            return value.T
        if r < c:
            return value
        if r < parts // 2:
            return jnp.where(upper, value, value.T)
        line = parts - 1 - r
        return jnp.where(diagonal, extra[line:line + 1, :], jnp.where(upper, value.T, value))

    trace = extra + sum(
        jnp.sum(jnp.where(diagonal, packed[at(place[p, p], FOLD), :], 0.0).reshape(-1, EXTRA, LANES), axis=0)
        for p in range(parts // 2)
    )
    trace = jnp.sum(jnp.sum(trace, axis=1, keepdims=True), axis=0, keepdims=True)
    inverse = 1.0 / (jnp.sqrt(trace) + 1e-07)
    inverse_sq = inverse * inverse

    def store_left(target, rows, c, high, low):
        for k, part in enumerate((high, low, high)):
            target[rows, k * hid + c * BLOCK:k * hid + (c + 1) * BLOCK] = part

    def store_right(target, r, c, high, low):
        for k, part in enumerate((high, high, low)):
            target[k * hid + r * BLOCK:k * hid + (r + 1) * BLOCK, at(c, BLOCK)] = part

    def store(left, right, r, c, value):
        high, low = split(value)
        places = [(r, c, high, low)] + ([(c, r, high.T, low.T)] if r != c else [])
        for i, j, first, second in places:
            if left is not None:
                store_left(left, at(i, BLOCK), j, first, second)
            if right is not None:
                store_right(right, i, j, first, second)

    def symmetric(left, right, r, c):
        halves = [left[r * BLOCK + k * FOLD:r * BLOCK + (k + 1) * FOLD, :] for k in range(per)]
        return jnp.concatenate([dot(half, right[:, at(c, BLOCK)], (1, 0)) for half in halves], axis=0)

    tall = columns // -(-columns // BLOCK)
    spans = [slice(begin, min(begin + tall, columns)) for begin in range(0, columns, tall)]

    def apply(left, right, c):
        for rows in spans:
            if left is None:
                yield rows, sum(
                    dot(part[rows, :], right[at(k, hid), at(c, BLOCK)], (1, 0))
                    for k, part in enumerate((given_high, given_low, given_high))
                )
            else:
                yield rows, dot(left[rows, :], right[:, at(c, BLOCK)], (1, 0))

    for r, c in pairs:
        rows = []
        for i in range(per):
            line = []
            for j in range(per):
                u, v = r * per + i, c * per + j
                line.append(piece(u, v))
            rows.append(jnp.concatenate(line, axis=1))
        value = jnp.concatenate(rows, axis=0) * inverse_sq
        gram[at(r, BLOCK), at(c, BLOCK)] = value
        store(al, ar, r, c, value)
    x, y = None, yl

    for number in range(ITERS - 1):
        for r, c in pairs:
            value = third_coef * symmetric(al, ar, r, c) + second_coef * gram[at(r, BLOCK), at(c, BLOCK)]
            store(None, pr, r, c, value + first_coef * eye if r == c else value)
        for r, c in pairs:
            store(tl, None, r, c, symmetric(al, pr, r, c))
        for c in range(blocks):
            for rows, value in apply(x, pr, c):
                if number == ITERS - 2:
                    x32[rows, at(c, BLOCK)] = value
                store_left(y, rows, c, *split(value))
        x, y = y, xl if y is yl else yl
        for r, c in pairs:
            value = symmetric(tl, pr, r, c)
            last = number == ITERS - 2
            store(None if last else al, ar, r, c, value)
            if not last:
                gram[at(r, BLOCK), at(c, BLOCK)] = value
    for c in range(blocks):
        for rows, value in apply(x, ar, c):
            y32[rows, at(c, BLOCK)] = value
            store_left(y, rows, c, *split(value))
    factor = inverse * scale
    for c in range(blocks):
        where = at(c, BLOCK)
        for rows, value in apply(y, ar, c):
            value = first_coef * x32[rows, where] + second_coef * y32[rows, where] + third_coef * value
            update[rows, where] = value * factor


def chain(cut, pieces, high, low, scale):
    columns, hid = high.shape
    vmem = pl.BlockSpec(memory_space=pltpu.VMEM)
    left, right = pltpu.VMEM((hid, 3 * hid), bf16), pltpu.VMEM((3 * hid, hid), bf16)
    slab, full = pltpu.VMEM((columns, 3 * hid), bf16), pltpu.VMEM((columns, hid), f32)
    return pl.pallas_call(
        functools.partial(chain_kernel, scale, cut, len(pieces)),
        in_specs=[vmem] * (2 + len(pieces)),
        out_specs=vmem,
        out_shape=jax.ShapeDtypeStruct((columns, hid), f32),
        scratch_shapes=[
            pltpu.VMEM((hid * hid // 2 // LANES, LANES), f32), pltpu.VMEM((hid, hid), f32),
            left, right, right, left, slab, slab, full, full,
        ],
        compiler_params=pltpu.CompilerParams(vmem_limit_bytes=46 * MIB),
    )(high, low, *pieces)


def body(local_grads, momentum):
    hid, wid = local_grads.shape[2:]
    rows = hid // STREAMS
    ways = [1 if k % 2 == 0 else -1 for k in range(STREAMS)]
    source = pltpu.with_memory_space_constraint(local_grads, pltpu.HBM)
    firsts = first_messages(source, "dp", ways, rows)
    terms = [transposed(source, "dp", way, k * rows, rows) for k, way in enumerate(ways)]
    grads = ring_sum_scatter("dp", ways, firsts, terms)
    squares = sum(jnp.sum((part * part).reshape(-1, 8, rows), axis=0) for part in grads)
    for line in (*two_lines("dp"), Line("expert", lax.axis_size("expert"), 1)):
        squares = line.sum(squares)
    cut = Cut(hid * hid // 2 // LANES, "dp")
    count = hid * wid * lax.axis_size("expert")
    factor, high, low, *parts = blend_gram(cut, count, squares, momentum[0].T, grads)
    new_momentum = momentum_decay * momentum[0].T + factor * jnp.concatenate(grads, axis=1)
    pieces = cut.all_sum(parts)
    update = chain(cut, pieces, high, low, 0.2 * math.sqrt(max(hid, wid)))
    return (new_momentum.T[None], update.T[None])


def solution(mesh):
    return jax.shard_map(
        body,
        mesh=mesh,
        in_specs=(P("expert", "dp", None, None), P("expert", None, "dp")),
        out_specs=(P("expert", None, "dp"), P("expert", None, "dp")),
        check_vma=False,
    )
```
